256 devices in a mesh: head: 8 (over y_lo, x), ctx: 32 (over z, y_hi, core).
Axes of the slice: x: 4, y: 4 (y_hi: 2, y_lo: 2; y = y_hi * 2 + y_lo), z: 8, core: 2. Of those that a mesh axis runs over, the one named last changes fastest.
Arguments:
- queries: bfloat16 [2048, 8192], P('ctx', 'head'), may hold values from -102 to 102
- latent_keys: bfloat16 [32768, 1024], P('ctx', 'head'), may hold values from -6 to 6
- latent_values: bfloat16 [32768, 1024], P('ctx', 'head'), may hold values from -6 to 6
- key_basis: bfloat16 [8, 128, 128], P('head'), may hold values from -0.5 to 0.5
- value_basis: bfloat16 [8, 128, 128], P('head'), may hold values from -0.5 to 0.5
- out_weight: bfloat16 [8192, 8192], P('head', 'ctx'), may hold values from -0.0625 to 0.0625
- positions: int32 [2048], replicated, may hold values from 0 to 32767, as said below
- key_segments: int32 [32768], replicated, may hold values from 0 to 1, as said below
Outputs:
- scored: bfloat16 [2048, 8192], P('head', 'ctx')
The draws below stay inside these ranges and needn't reach their ends.
Inputs may be any that keep to these rules, and one draw needn't show every extreme that they name: `positions`: strictly rising; rows c*64 to (c+1)*64 - 1 hold positions in c*1024 to (c+1)*1024 - 1. `key_segments`: never falling; each of the 2 values names one nonempty run of tokens.
All inputs are finite; a program needn't handle non-finite values.
Results may differ from the reference program's by a relative error of at most 0.012.
The reference program's roundings to bfloat16 on the way (of `keys`, `values`, `weights` and `attended`) count: a program that leaves them out, or rounds other values in their place, can miss the bound.
Values may be sent and summed in bfloat16 or wider, within the bound.
No kernel may reach another device: no remote copies, remote signals or barrier semaphores. Data moves between devices by JAX's collectives and lax.ppermute only.
A program may use at most 128 MiB of HBM per device.

```python
import jax
import jax.numpy as jnp
from jax import lax

D = 8192
HD = 128
R = 128
GROUP = 8
NSEG = 2
Q_DEV = 64
LC = 1024
KVH = 8
NQH = 64
QTOK = 2048
L = 32768


def trace_layout(key):
    cut_key = jax.random.fold_in(key, 101)
    place_key = jax.random.fold_in(key, 202)
    cuts = jnp.sort(jax.random.permutation(cut_key, L - 1)[:NSEG - 1] + 1)
    segments = jnp.sum((jnp.arange(L, dtype=jnp.int32)[:, None] >= cuts[None, :]).astype(jnp.int32), axis=1)
    shard_count = QTOK // Q_DEV
    block_keys = jax.random.split(place_key, shard_count)
    offsets = jax.vmap(lambda one_key: jnp.sort(jax.random.permutation(one_key, LC)[:Q_DEV]))(block_keys)
    offsets = offsets.astype(jnp.int32)
    offsets = offsets.at[0, 0].set(0)
    offsets = offsets.at[shard_count - 1, Q_DEV - 1].set(LC - 1)
    places = offsets + LC * jnp.arange(shard_count, dtype=jnp.int32)[:, None]
    return (places.reshape(QTOK).astype(jnp.int32), segments.astype(jnp.int32))


def draw_positions(key, part):
    places, segments = trace_layout(key)
    return places


def draw_key_segments(key, part):
    places, segments = trace_layout(key)
    return segments


def draw_queries(key, part):
    key = jax.random.fold_in(key, 11)
    noise_key = jax.random.fold_in(key, 1)
    shape = (QTOK, GROUP * KVH * HD)
    values = jnp.clip(jax.random.normal(noise_key, shape, jnp.float32), -6.0, 6.0)
    return values.astype(jnp.bfloat16)


def level_of(key, dims, shards, smallest, largest):
    def one(position, blocks):
        heights = jax.random.uniform(jax.random.fold_in(jax.random.fold_in(key, 6), position), (blocks,), jnp.float32, smallest / len(shards), largest / len(shards))
        return jnp.repeat(jnp.exp(heights), dims[position] // blocks).reshape((-1,) + (1,) * (len(dims) - position - 1))

    factor_of = one(*shards[0])
    for cut in shards[1:]:
        factor_of = factor_of * one(*cut)
    return factor_of


def gaussian(stream_key, extent, scale, bound, cuts=(), kind=jnp.bfloat16):
    values = jax.random.normal(stream_key, extent, jnp.float32) * scale
    if len(cuts) > 0:
        values = level_of(stream_key, extent, cuts, -0.22, 0.18) * values
    return jnp.clip(values, min=-bound, max=bound).astype(kind)


def setup_inputs(seed: int = 0) -> dict:
    seeds = jax.random.split(jax.random.key(seed), 9)
    queries = draw_queries(jax.random.fold_in(seeds[8], 71), 0)
    latent_keys = gaussian(seeds[1], (L, KVH * R), 1.0, 6.0, ((0, 32), (1, 8)))
    latent_values = gaussian(seeds[2], (L, KVH * R), 1.0, 6.0, ((0, 32), (1, 8)))
    key_basis = gaussian(seeds[3], (KVH, R, HD), R ** -0.5, 0.5, ((0, 8),))
    value_basis = gaussian(seeds[4], (KVH, R, HD), R ** -0.5, 0.5, ((0, 8),))
    out_weight = gaussian(seeds[5], (NQH * HD, D), (NQH * HD) ** -0.5, 0.0625, ((0, 8), (1, 32)))
    positions = draw_positions(jax.random.fold_in(seeds[8], 71), 0)
    key_segments = draw_key_segments(jax.random.fold_in(seeds[8], 71), 0)
    return {"queries": queries, "latent_keys": latent_keys, "latent_values": latent_values, "key_basis": key_basis, "value_basis": value_basis, "out_weight": out_weight, "positions": positions, "key_segments": key_segments}


masked_score = -1e30


def reference(queries, latent_keys, latent_values, key_basis, value_basis, out_weight, positions, key_segments):
    query_steps = key_segments[positions]
    key_place = jnp.arange(L, dtype=jnp.int32)
    block_rows = min(256, QTOK)
    blocks = QTOK // block_rows
    scale = HD ** -0.5

    def one_head(index):
        lat_k = lax.dynamic_slice_in_dim(latent_keys, index * R, R, 1)
        lat_v = lax.dynamic_slice_in_dim(latent_values, index * R, R, 1)
        keys = jnp.dot(lat_k, key_basis[index], preferred_element_type=jnp.float32).astype(jnp.bfloat16)
        values = jnp.dot(lat_v, value_basis[index], preferred_element_type=jnp.float32).astype(jnp.bfloat16)
        keys = lax.optimization_barrier(keys).astype(jnp.float32)
        values = lax.optimization_barrier(values).astype(jnp.float32)
        head_q = lax.dynamic_slice_in_dim(queries, index * GROUP * HD, GROUP * HD, 1)
        head_q = head_q.reshape(blocks, block_rows, GROUP, HD)

        def block(items):
            query_block, place_block, step_block = items
            scores = jnp.einsum("qgd,kd->qgk", query_block.astype(jnp.float32), keys) * scale
            allowed = (key_place[None, :] <= place_block[:, None]) & (key_segments[None, :] == step_block[:, None])
            scores = jnp.where(allowed[:, None, :], scores, masked_score)
            top = jnp.max(scores, axis=-1, keepdims=True)
            raw = jnp.where(allowed[:, None, :], jnp.exp(scores - top), 0.0)
            total = jnp.sum(raw, axis=-1)
            weights = lax.optimization_barrier(raw.astype(jnp.bfloat16)).astype(jnp.float32)
            summed = jnp.einsum("qgk,kd->qgd", weights, values)
            return (summed / total[..., None]).astype(jnp.bfloat16).reshape(block_rows, GROUP * HD)

        return lax.map(block, (head_q, positions.reshape(blocks, block_rows), query_steps.reshape(blocks, block_rows)))

    attended = lax.map(one_head, jnp.arange(KVH, dtype=jnp.int32))
    attended = jnp.transpose(attended, (1, 2, 0, 3)).reshape(QTOK, KVH * GROUP * HD)
    return jnp.dot(attended, out_weight, preferred_element_type=jnp.float32).astype(jnp.bfloat16)
```

```python
import functools
import math

import jax
import jax.numpy as jnp
import numpy as np
from jax import lax
from jax.experimental import pallas as pl
from jax.experimental.pallas import tpu as pltpu
from jax.sharding import Mesh, PartitionSpec as P

NZ = 8
FLOOR = -1e30
MASKED = -2e38
F32 = jnp.float32
BF16 = jnp.bfloat16
VMEM = pl.BlockSpec(memory_space=pltpu.VMEM)
SMEM = pl.BlockSpec(memory_space=pltpu.SMEM)
ANY = pl.BlockSpec(memory_space=pl.ANY)
LIMIT = 48 * 1024 * 1024
MATE = [(z + 1) % NZ if z % 2 else (z - 1) % NZ for z in range(NZ)]
SHIFTS = (0, 2, 6, 4)


def cost(flops, moved):
    return pl.CostEstimate(flops=int(flops), bytes_accessed=int(moved), transcendentals=0)


def rebuild_kernel(lk_ref, lv_ref, bk_ref, bv_ref, kv_ref):
    hd = bk_ref.shape[2]
    kv_ref[:, :hd] = jnp.dot(lk_ref[...], bk_ref[0], preferred_element_type=F32).astype(BF16)
    kv_ref[:, hd:] = jnp.dot(lv_ref[...], bv_ref[0], preferred_element_type=F32).astype(BF16)


def rebuild(lk, lv, bk, bv):
    rows, hd = lk.shape[0], bk.shape[2]
    return pl.pallas_call(
        rebuild_kernel,
        out_shape=jax.ShapeDtypeStruct((rows, 2 * hd), BF16),
        in_specs=[VMEM] * 4,
        out_specs=VMEM,
        compiler_params=pltpu.CompilerParams(vmem_limit_bytes=LIMIT),
        cost_estimate=cost(4 * rows * hd * hd, 8 * rows * hd),
    )(lk, lv, bk, bv)


def flash_kernel(nq, nk, first, last, groups, rows, scale2, row_chunk, *refs):
    ids, pos_ref = refs[0], refs[1]
    qs = refs[2 : 2 + nq]
    kvs = refs[2 + nq : 2 + nq + nk]
    at = 2 + nq + nk
    if not first:
        state_in = refs[at : at + 3]
        at += 3
    outs_n = nq if last else 3
    outs = refs[at : at + outs_n]
    at += outs_n
    q_s, kv_s, pos_s, m_s, l_s, acc_s, q_sem, kv_sem, st_sem = refs[at : at + 9]
    hd = kvs[0].shape[1] // 2
    span = kvs[0].shape[0]
    tokens = qs[0].shape[0]
    kv_copies = [pltpu.make_async_copy(kvs[j], kv_s.at[j], kv_sem.at[j]) for j in range(nk)]
    q_copies = [
        [
            pltpu.make_async_copy(
                qs[i].at[:, pl.ds(g * hd, hd)],
                q_s.at[i, pl.ds(g * tokens, tokens), :],
                q_sem.at[i, g],
            )
            for g in range(groups)
        ]
        for i in range(nq)
    ]
    for i in range(nq):
        for c in q_copies[i]:
            c.start()
    for c in kv_copies:
        c.start()
    if first:
        m_s[...] = jnp.full_like(m_s, FLOOR)
        l_s[...] = jnp.zeros_like(l_s)
        acc_s[...] = jnp.zeros_like(acc_s)
    else:
        st_copies = [
            pltpu.make_async_copy(state_in[n], (m_s, l_s, acc_s)[n], st_sem.at[n]) for n in range(3)
        ]
        for c in st_copies:
            c.start()
    cut = ids[nq + nk]
    spot = lax.broadcasted_iota(jnp.int32, (tokens, tokens), 0) == lax.broadcasted_iota(
        jnp.int32, (tokens, tokens), 1
    )
    for i in range(nq):
        row = pos_ref[pl.ds(ids[i], 1), :].astype(F32)
        col = jnp.sum(jnp.where(spot, jnp.broadcast_to(row, (tokens, tokens)), 0.0), axis=1, keepdims=True)
        wide = jnp.broadcast_to(col, (tokens, hd)).astype(jnp.int32)
        for g in range(groups):
            pos_s[i, g * tokens : (g + 1) * tokens, :] = wide
    for i in range(nq):
        for c in q_copies[i]:
            c.wait()
    if not first:
        for c in st_copies:
            c.wait()
    for c in kv_copies:
        c.wait()

    def unit(i, j, r0, masked, cq, ck):
        at_rows = pl.ds(r0, row_chunk)
        q = q_s[i, at_rows, :]
        k = kv_s[j, :, :hd]
        v = kv_s[j, :, hd:]
        s = lax.dot_general(q, k, (((1,), (1,)), ((), ())), preferred_element_type=F32)
        if masked:
            kpos = lax.broadcasted_iota(jnp.int32, (row_chunk, span), 1) + ck * span
            pos = pos_s[i, at_rows, :][:, :1]
            low = jnp.where(pos >= cut, cut, 0)
            s = jnp.where((kpos <= pos) & (kpos >= low), s, MASKED)
        m_old = m_s[i, at_rows, :]
        m_new = jnp.maximum(m_old, jnp.max(s, axis=1, keepdims=True))
        fade = jnp.exp2((m_old - m_new) * scale2)
        shift = (m_new * scale2)[:, :1]
        p = jnp.exp2(s * scale2 - shift)
        part = p[:, :hd]
        for t in range(1, span // hd):
            part = part + p[:, t * hd : (t + 1) * hd]
        l_s[i, at_rows, :] = l_s[i, at_rows, :] * fade + part
        acc_s[i, at_rows, :] = acc_s[i, at_rows, :] * fade + jnp.dot(
            p.astype(BF16), v, preferred_element_type=F32
        )
        m_s[i, at_rows, :] = m_new

    def one(n, carry):
        i = n // nk
        j = n % nk
        cq = ids[i]
        ck = ids[nq + j]
        begin_k, end_k = ck * span, (ck + 1) * span
        begin_q, end_q = cq * span, (cq + 1) * span
        apart = (cut >= end_k) & (cut <= begin_q)
        whole = (ck < cq) & ((cut <= begin_k) | (cut >= end_q))
        some = (ck <= cq) & jnp.logical_not(apart) & jnp.logical_not(whole)

        @pl.when(whole)
        def _():
            for r in range(rows // row_chunk):
                unit(i, j, r * row_chunk, False, cq, ck)

        @pl.when(some)
        def _():
            for r in range(rows // row_chunk):
                unit(i, j, r * row_chunk, True, cq, ck)

        return carry

    lax.fori_loop(0, nq * nk, one, 0)
    if not last:
        out_copies = [
            pltpu.make_async_copy((m_s, l_s, acc_s)[n], outs[n], st_sem.at[n]) for n in range(3)
        ]
        for c in out_copies:
            c.start()
        for c in out_copies:
            c.wait()
        return
    lane = lax.broadcasted_iota(jnp.int32, (tokens, hd), 1)
    for i in range(nq):
        stat = jnp.zeros((tokens, hd), F32)
        for g in range(groups):
            at_rows = pl.ds(g * tokens, tokens)
            total = jnp.sum(l_s[i, at_rows, :], axis=1, keepdims=True)
            used = total > 0.0
            safe = jnp.where(used, total, 1.0)
            outs[i][:, g * hd : (g + 1) * hd] = (acc_s[i, at_rows, :] / safe).astype(BF16)
            level = jnp.where(used, m_s[i, at_rows, :] * scale2 + jnp.log2(safe), FLOOR)
            high = level.astype(BF16).astype(F32)
            mid = (level - high).astype(BF16).astype(F32)
            low = level - high - mid
            flag = jnp.where(used, 1.0, 0.0)
            stat = jnp.where(lane == g, high, stat)
            stat = jnp.where(lane == groups + g, mid, stat)
            stat = jnp.where(lane == 2 * groups + g, low, stat)
            stat = jnp.where(lane == 3 * groups + g, flag, stat)
        outs[i][:, groups * hd :] = stat.astype(BF16)


def flash(ids, pos, qs, kvs, state, last, row_chunk=256):
    nq, nk = len(qs), len(kvs)
    tokens, width = qs[0].shape
    span, hd = kvs[0].shape[0], kvs[0].shape[1] // 2
    groups = width // hd
    rows = groups * tokens
    scale2 = math.log2(math.e) * hd ** (-0.5)
    first = state is None
    acc = jax.ShapeDtypeStruct((nq, rows, hd), F32)
    if last:
        outs = [jax.ShapeDtypeStruct((tokens, width + hd), BF16)] * nq
        out_specs = [VMEM] * nq
    else:
        outs = [acc] * 3
        out_specs = [ANY] * 3
    body = functools.partial(
        flash_kernel, nq, nk, first, last, groups, rows, scale2, row_chunk
    )
    return pl.pallas_call(
        body,
        out_shape=outs,
        in_specs=[SMEM, VMEM] + [ANY] * (nq + nk + (0 if first else 3)),
        out_specs=out_specs,
        scratch_shapes=[
            pltpu.VMEM((nq, rows, hd), BF16),
            pltpu.VMEM((nk, span, 2 * hd), BF16),
            pltpu.VMEM((nq, rows, hd), jnp.int32),
            pltpu.VMEM((nq, rows, hd), F32),
            pltpu.VMEM((nq, rows, hd), F32),
            pltpu.VMEM((nq, rows, hd), F32),
            pltpu.SemaphoreType.DMA((nq, groups)),
            pltpu.SemaphoreType.DMA((nk,)),
            pltpu.SemaphoreType.DMA((3,)),
        ],
        compiler_params=pltpu.CompilerParams(vmem_limit_bytes=LIMIT),
        cost_estimate=cost(4 * nq * rows * nk * span * hd * 0.6 * 4, nk * span * hd * 4),
    )(ids, pos, *qs, *kvs, *(() if first else state))


def combine_kernel(groups, *refs):
    parts, out = refs[:-1], refs[-1]
    tokens, width = out.shape
    hd = width // groups
    stats = [r[:, width:].astype(F32) for r in parts]
    for g in range(groups):
        levels = []
        for s in stats:
            level = (
                s[:, g : g + 1]
                + s[:, groups + g : groups + g + 1]
                + s[:, 2 * groups + g : 2 * groups + g + 1]
            )
            levels.append(jnp.where(s[:, 3 * groups + g : 3 * groups + g + 1] > 0.0, level, FLOOR))
        top = functools.reduce(jnp.maximum, levels)
        shares = [jnp.where(x > FLOOR, jnp.exp2(x - top), 0.0) for x in levels]
        total = functools.reduce(lambda a, b: a + b, shares)
        summed = 0.0
        for r, share in zip(parts, shares):
            summed = summed + r[:, g * hd : (g + 1) * hd].astype(F32) * share
        out[:, g * hd : (g + 1) * hd] = (summed / total).astype(BF16)


def combine(parts, groups):
    tokens, wide = parts[0].shape
    hd = wide // (groups + 1)
    return pl.pallas_call(
        functools.partial(combine_kernel, groups),
        out_shape=jax.ShapeDtypeStruct((tokens, groups * hd), BF16),
        in_specs=[VMEM] * len(parts),
        out_specs=VMEM,
        compiler_params=pltpu.CompilerParams(vmem_limit_bytes=LIMIT),
        cost_estimate=cost(1e6, 1e6),
    )(*parts)


def project_kernel(nb, nw, *refs):
    ids = refs[0]
    blocks = refs[1 : 1 + nb]
    ws = refs[1 + nb : 1 + nb + nw]
    outs = refs[1 + nb + nw : -1]
    rows_s = refs[-1]
    tokens = blocks[0].shape[0]
    cols = ws[0].shape[1]
    for b in range(nb):
        rows_s[pl.ds(pl.multiple_of(ids[b] * tokens, tokens), tokens), :] = blocks[b][...]
    rows = rows_s[...]
    for w in range(nw):
        y = jnp.dot(rows, ws[w][...], preferred_element_type=F32).astype(BF16)
        for n, out in enumerate(outs):
            for half in range(2):
                lo = (2 * n + half) * tokens
                out[half, :, w * cols : (w + 1) * cols] = y[lo : lo + tokens]


def project(slots, blocks, ws, nx):
    tokens, width = blocks[0].shape
    nb, nw = len(blocks), len(ws)
    cols = ws[0].shape[1]
    out = jax.ShapeDtypeStruct((2, tokens, nw * cols), BF16)
    return pl.pallas_call(
        functools.partial(project_kernel, nb, nw),
        out_shape=[out] * nx,
        in_specs=[SMEM] + [VMEM] * (nb + nw),
        out_specs=[VMEM] * nx,
        scratch_shapes=[pltpu.VMEM((nb * tokens, width), BF16)],
        compiler_params=pltpu.CompilerParams(vmem_limit_bytes=LIMIT),
        cost_estimate=cost(2 * nb * tokens * width * nw * cols, 4e6),
    )(slots, *blocks, *ws)


def swap(array, axis):
    return lax.ppermute(array, axis, [(0, 1), (1, 0)])


def to_mate(array):
    return lax.ppermute(array, "z", [(z, MATE[z]) for z in range(NZ)])


def useful(plane, owner):
    return owner >= min(plane, MATE[plane])


def fetch(array, k, trim):
    pairs = [((z + k) % NZ, z) for z in range(NZ) if not trim or useful(z, (z + k) % NZ)]
    return lax.ppermute(array, "z", pairs)


def give(array, k):
    pairs = [(z, (z + k) % NZ) for z in range(NZ) if useful(z, (z + k) % NZ)]
    return lax.ppermute(array, "z", pairs)


def per_device(
    queries, latent_keys, latent_values, key_basis, value_basis, out_weight, positions, key_segments
):
    z, yh, core = lax.axis_index("z"), lax.axis_index("yh"), lax.axis_index("core")
    yl, x = lax.axis_index("yl"), lax.axis_index("x")
    tokens, width = queries.shape
    hd = key_basis.shape[2]
    groups = width // hd
    span = latent_keys.shape[0]
    qs = [queries] + [fetch(queries, k, True) for k in SHIFTS[1:]]
    kv = rebuild(latent_keys, latent_values, key_basis, value_basis)
    kv_mate = to_mate(kv)
    kv_y = swap(kv, "yh")
    kv_mate_y = swap(kv_mate, "yh")
    own = [kv, swap(kv, "core"), kv_y, swap(kv_y, "core")]
    far = [kv_mate, swap(kv_mate, "core"), kv_mate_y, swap(kv_mate_y, "core")]
    w_y = swap(out_weight, "yh")
    ws = [out_weight, swap(out_weight, "core"), w_y, swap(w_y, "core")]

    mate = jnp.where(z % 2 == 1, (z + 1) % NZ, (z + NZ - 1) % NZ)
    cut = span * 4 * NZ - jnp.sum(key_segments)
    place = 2 * yh + core
    qids = [4 * ((z + k) % NZ) + place for k in SHIFTS]
    near = [2 * (yh ^ a) + (core ^ b) for a in (0, 1) for b in (0, 1)]
    pos = positions.reshape(-1, tokens)
    ids_own = jnp.stack(qids + [4 * z + n for n in near] + [cut]).astype(jnp.int32)
    ids_far = jnp.stack(qids + [4 * mate + n for n in near] + [cut]).astype(jnp.int32)
    state = flash(ids_own, pos, qs, own, None, False)
    parts = flash(ids_far, pos, qs, far, state, True)

    back = [parts[0]] + [give(part, k) for part, k in zip(parts[1:], SHIFTS[1:])]
    attended = combine(back, groups)

    blocks = [attended] + [fetch(attended, k, False) for k in SHIFTS[1:]]
    mates = to_mate(jnp.concatenate(blocks, axis=0))
    blocks = blocks + [mates[n * tokens : (n + 1) * tokens] for n in range(4)]
    planes = [(z + k) % NZ for k in SHIFTS] + [(mate + k) % NZ for k in SHIFTS]
    slots = [2 * ((p % 4 - x) % 4) + ((p // 4) ^ yl) for p in planes]
    outs = project(jnp.stack(slots).astype(jnp.int32), blocks, ws, 4)

    def along_x(array, k):
        return lax.ppermute(array, "x", [(n, (n + k) % 4) for n in range(4)])

    summed = outs[0].astype(F32)
    for k in (1, 2, 3):
        summed = summed + along_x(outs[k], k).astype(F32)
    half = summed.shape[2] // 2

    def along_y(array, a, b):
        pairs = [(2 * m + n, 2 * (m ^ a) + (n ^ b)) for m in range(2) for n in range(2)]
        return lax.ppermute(array, ("yl", "yh"), pairs)

    sent = summed.astype(BF16)
    from_l = along_y(sent[1, :, :half], 1, 0)
    from_h = along_y(sent[0, :, half:], 0, 1)
    from_lh = along_y(sent[1, :, half:], 1, 1)
    mine = (summed[0, :, :half] + from_l.astype(F32)).astype(BF16)
    theirs = (from_h.astype(F32) + from_lh.astype(F32)).astype(BF16)
    both = jnp.stack([jnp.where(yh == 0, mine, theirs), jnp.where(yh == 0, theirs, mine)])
    cols = half // 2
    here = both[:, :, :cols]
    there = swap(both[:, :, cols:], "core")
    rows = jnp.stack([jnp.where(core == 0, here, there), jnp.where(core == 0, there, here)], axis=1)
    return rows.reshape(-1, cols)


def solution(mesh):
    fine = Mesh(mesh.devices.reshape(2, 4, NZ, 2, 2), ("yl", "x", "z", "yh", "core"))
    head, ctx = ("yl", "x"), ("z", "yh", "core")
    placed = (
        P(ctx, head),
        P(ctx, head),
        P(ctx, head),
        P(head, None, None),
        P(head, None, None),
        P(head, ctx),
        P(),
        P(),
    )
    return jax.shard_map(
        per_device, mesh=fine, in_specs=placed, out_specs=P(head, ctx), check_vma=False
    )
```

```python
import functools
import math

import jax
import jax.numpy as jnp
import numpy as np
from jax import lax
from jax.experimental import pallas as pl
from jax.experimental.pallas import tpu as pltpu
from jax.sharding import Mesh, PartitionSpec as P

NZ = 8
FLOOR = -1e30
MASKED = -2e38
CLIMB = 40.0
F32 = jnp.float32
BF16 = jnp.bfloat16
VMEM = pl.BlockSpec(memory_space=pltpu.VMEM)
SMEM = pl.BlockSpec(memory_space=pltpu.SMEM)
ANY = pl.BlockSpec(memory_space=pl.ANY)
LIMIT = 24 * 1024 * 1024
FLASH_LIMIT = 60 * 1024 * 1024
SHIFTS = (0, 2, 6, 4)


def cost(flops, moved):
    return pl.CostEstimate(flops=int(flops), bytes_accessed=int(moved), transcendentals=0)


def rebuild_kernel(lk_in, lv_in, bk_in, bv_in, kv_ref, lk_ref, lv_ref, bk_ref, bv_ref, sems):
    pairs = [(lk_in, lk_ref), (bk_in, bk_ref), (lv_in, lv_ref), (bv_in, bv_ref)]
    copies = [pltpu.make_async_copy(a, b, sems.at[n]) for n, (a, b) in enumerate(pairs)]
    for c in copies:
        c.start()
    for c in copies:
        c.wait()
    hd = bk_ref.shape[2]
    values = lax.dot_general(
        bv_ref[0], lv_ref[...], (((0,), (1,)), ((), ())), preferred_element_type=F32
    )
    kv_ref[:hd, :] = values.astype(BF16)
    for t in range(lk_ref.shape[0] // hd):
        part = slice(t * hd, (t + 1) * hd)
        keys = jnp.dot(lk_ref[part, :], bk_ref[0], preferred_element_type=F32)
        kv_ref[hd:, part] = keys.astype(BF16)


def rebuild(lk, lv, bk, bv):
    rows, hd = lk.shape[0], bk.shape[2]
    arrays = (lk, lv, bk, bv)
    return pl.pallas_call(
        rebuild_kernel,
        out_shape=jax.ShapeDtypeStruct((2 * hd, rows), BF16),
        in_specs=[ANY] * 4,
        out_specs=VMEM,
        scratch_shapes=[pltpu.VMEM(t.shape, t.dtype) for t in arrays]
        + [pltpu.SemaphoreType.DMA((4,))],
        compiler_params=pltpu.CompilerParams(vmem_limit_bytes=FLASH_LIMIT),
        cost_estimate=cost(4 * rows * hd * hd, 8 * rows * hd),
    )(*arrays)


def flash_kernel(nq, nk, first, last, groups, rows, scale2, *refs):
    ids, pos_ref = refs[0], refs[1]
    qs = refs[2 : 2 + nq]
    kvs = refs[2 + nq : 2 + nq + nk]
    at = 2 + nq + nk
    if not first:
        held = refs[at : at + 3 * nq]
        at += 3 * nq
    if last:
        outs = refs[at : at + nq]
        at += nq
    else:
        outs = refs[at : at + 3 * nq]
        at += 3 * nq
    flat_s, q_s, kv_s, pos_s, acc_t, begun, todo, m_s, l_s, acc_s, q_sem, kv_sem, st_sem = refs[
        at:
    ]
    hd = kvs[0].shape[0] // 2
    span = kvs[0].shape[1]
    tokens = qs[0].shape[0]
    kv_copies = [pltpu.make_async_copy(kvs[j], kv_s.at[j], kv_sem.at[j]) for j in range(nk)]
    q_copies = [pltpu.make_async_copy(qs[i], flat_s.at[i], q_sem.at[i]) for i in range(nq)]
    for c in q_copies:
        c.start()
    for c in kv_copies:
        c.start()
    if first:
        m_s[...] = jnp.full_like(m_s, FLOOR)
        l_s[...] = jnp.zeros_like(l_s)
        acc_s[...] = jnp.zeros_like(acc_s)
    else:
        held_copies = [
            pltpu.make_async_copy(r, (m_s, l_s, acc_s)[n % 3].at[n // 3], st_sem.at[n])
            for n, r in enumerate(held)
        ]
        for c in held_copies:
            c.start()
    cut = ids[nq + nk]
    for i in range(nq):
        row = pos_ref[pl.ds(ids[i], 1), :]
        pos_s[i] = jnp.broadcast_to(jnp.concatenate([row] * groups, axis=1), (8, rows))
    for i in range(nq):
        q_copies[i].wait()
        for g in range(groups):
            q_s[i, g * tokens : (g + 1) * tokens, :] = flat_s[i, :, g * hd : (g + 1) * hd]
    if not first:
        for c in held_copies:
            c.wait()

    def scores_of(i, j, step):
        out = []
        for t in range(0, span, step):
            k = jnp.concatenate(
                [kv_s[j, hd:, u : u + hd] for u in range(t, t + step, hd)], axis=0
            )
            out.append(
                lax.dot_general(k, q_s[i], (((1,), (1,)), ((), ())), preferred_element_type=F32)
            )
        return out

    def safe_unit(i, j, ck):
        (s,) = scores_of(i, j, span)
        kpos = lax.broadcasted_iota(jnp.int32, (span, rows), 0) + ck * span
        pos = pos_s[i, :1, :]
        low = jnp.where(pos >= cut, cut, 0)
        s = jnp.where((kpos <= pos) & (kpos >= low), s, MASKED)
        s = s.reshape(span // 8, 8, rows)
        m_old = m_s[i]
        m_new = jnp.maximum(m_old, jnp.max(jnp.max(s, axis=0), axis=0, keepdims=True))
        fade = jnp.exp2((m_old - m_new) * scale2)
        p = jnp.exp2(s * scale2 - (m_new * scale2)[None])
        l_s[i] = l_s[i] * fade + jnp.sum(p, axis=0)
        acc_s[i] = acc_s[i] * fade[:1] + jnp.dot(
            kv_s[j, :hd, :], p.reshape(span, rows).astype(BF16), preferred_element_type=F32
        )
        m_s[i] = m_new

    def fast_unit(i, j):
        step = 2 * hd
        m_old = m_s[i]
        base = m_old * scale2
        top = m_old
        total = l_s[i]
        parts = []
        for s in scores_of(i, j, step):
            s = s.reshape(step // 8, 8, rows)
            top = jnp.maximum(top, jnp.max(s, axis=0))
            p = jnp.exp2(s * scale2 - base[None])
            total = total + jnp.sum(p, axis=0)
            parts.append(p.reshape(step, rows).astype(BF16))
        acc_t[...] = acc_s[i] + jnp.dot(
            kv_s[j, :hd, :], jnp.concatenate(parts, axis=0), preferred_element_type=F32
        )
        m_new = jnp.broadcast_to(jnp.max(top, axis=0, keepdims=True), (8, rows))
        climb = (m_new - m_old) * scale2
        fine = jnp.max(climb) < CLIMB

        @pl.when(fine)
        def _():
            fade = jnp.exp2(-climb)
            l_s[i] = total * fade
            acc_s[i] = acc_t[...] * fade[:1]
            m_s[i] = m_new

        return fine

    for i in range(nq):
        begun[i] = (jnp.max(m_s[i]) > 0.5 * FLOOR).astype(jnp.int32) if not first else jnp.int32(0)

    def one(n, carry):
        j = n // nq
        i = n % nq
        cq = ids[i]
        ck = ids[nq + j]
        begin_k, end_k = ck * span, (ck + 1) * span
        begin_q, end_q = cq * span, (cq + 1) * span
        apart = (cut >= end_k) & (cut <= begin_q)
        whole = (ck < cq) & ((cut <= begin_k) | (cut >= end_q))
        some = (ck <= cq) & jnp.logical_not(apart)
        todo[0] = some.astype(jnp.int32)

        @pl.when(i == 0)
        def _():
            pltpu.make_async_copy(kv_s.at[j], kv_s.at[j], kv_sem.at[j]).wait()

        @pl.when(whole & (begun[i] == 0))
        def _():
            s = lax.dot_general(
                kv_s[j, hd:, :hd], q_s[i], (((1,), (1,)), ((), ())), preferred_element_type=F32
            )
            m_s[i] = jnp.broadcast_to(jnp.max(s, axis=0, keepdims=True), (8, rows))
            begun[i] = 1

        @pl.when(whole)
        def _():
            todo[0] = 1 - fast_unit(i, j).astype(jnp.int32)

        @pl.when(todo[0] > 0)
        def _():
            safe_unit(i, j, ck)
            begun[i] = 1

        return carry

    lax.fori_loop(0, nq * nk, one, 0)
    if not last:
        out_copies = [
            pltpu.make_async_copy((m_s, l_s, acc_s)[n % 3].at[n // 3], r, st_sem.at[n])
            for n, r in enumerate(outs)
        ]
        for c in out_copies:
            c.start()
        for c in out_copies:
            c.wait()
        return
    lane = lax.broadcasted_iota(jnp.int32, (tokens, hd), 1)
    for i in range(nq):
        total = jnp.sum(l_s[i], axis=0, keepdims=True)
        used = total > 0.0
        safe = jnp.where(used, total, 1.0)
        done = acc_s[i] * (1.0 / safe)
        level = jnp.where(used, m_s[i, :1, :] * scale2 + jnp.log2(safe), FLOOR)
        high = level.astype(BF16).astype(F32)
        mid = (level - high).astype(BF16).astype(F32)
        low = level - high - mid
        flag = jnp.where(used, 1.0, 0.0)
        stats = [high, mid, low, flag]
        table = jnp.concatenate(
            [v[:, g * tokens : (g + 1) * tokens] for v in stats for g in range(groups)]
            + [jnp.zeros((hd - 4 * groups, tokens), F32)],
            axis=0,
        )
        outs[i][:, groups * hd :] = table.T.astype(BF16)
        for g in range(groups):
            block = done[:, g * tokens : (g + 1) * tokens]
            outs[i][:, g * hd : (g + 1) * hd] = block.T.astype(BF16)


def flash(ids, pos, qs, kvs, state, last):
    nq, nk = len(qs), len(kvs)
    tokens, width = qs[0].shape
    hd, span = kvs[0].shape[0] // 2, kvs[0].shape[1]
    groups = width // hd
    rows = groups * tokens
    scale2 = math.log2(math.e) * hd ** (-0.5)
    first = state is None
    state_types = [
        jax.ShapeDtypeStruct((8, rows), F32),
        jax.ShapeDtypeStruct((8, rows), F32),
        jax.ShapeDtypeStruct((hd, rows), F32),
    ]
    scratch = [
        pltpu.VMEM((nq, tokens, width), BF16),
        pltpu.VMEM((nq, rows, hd), BF16),
        pltpu.VMEM((nk, 2 * hd, span), BF16),
        pltpu.VMEM((nq, 8, rows), jnp.int32),
        pltpu.VMEM((hd, rows), F32),
        pltpu.SMEM((nq,), jnp.int32),
        pltpu.SMEM((1,), jnp.int32),
    ]
    scratch += [pltpu.VMEM((nq, *t.shape), t.dtype) for t in state_types]
    if last:
        outs = [jax.ShapeDtypeStruct((tokens, width + hd), BF16)] * nq
    else:
        outs = state_types * nq
    scratch += [
        pltpu.SemaphoreType.DMA((nq,)),
        pltpu.SemaphoreType.DMA((nk,)),
        pltpu.SemaphoreType.DMA((3 * nq,)),
    ]
    return pl.pallas_call(
        functools.partial(flash_kernel, nq, nk, first, last, groups, rows, scale2),
        out_shape=outs,
        in_specs=[SMEM, VMEM] + [ANY] * (nq + nk + (0 if first else 3 * nq)),
        out_specs=[VMEM if last else ANY] * len(outs),
        scratch_shapes=scratch,
        compiler_params=pltpu.CompilerParams(vmem_limit_bytes=FLASH_LIMIT),
        cost_estimate=cost(4 * nq * rows * nk * span * hd * 0.6 * 4, nk * span * hd * 4),
    )(ids, pos, *qs, *kvs, *(() if first else state))


def combine_kernel(groups, *refs):
    parts, out = refs[:-1], refs[-1]
    tokens, width = out.shape
    hd = width // groups
    stats = [r[:, width:].astype(F32) for r in parts]
    for g in range(groups):
        levels = []
        for s in stats:
            level = (
                s[:, g : g + 1]
                + s[:, groups + g : groups + g + 1]
                + s[:, 2 * groups + g : 2 * groups + g + 1]
            )
            levels.append(jnp.where(s[:, 3 * groups + g : 3 * groups + g + 1] > 0.0, level, FLOOR))
        top = functools.reduce(jnp.maximum, levels)
        shares = [jnp.where(x > FLOOR, jnp.exp2(x - top), 0.0) for x in levels]
        total = functools.reduce(lambda a, b: a + b, shares)
        summed = 0.0
        for r, share in zip(parts, shares):
            summed = summed + r[:, g * hd : (g + 1) * hd].astype(F32) * share
        out[:, g * hd : (g + 1) * hd] = (summed / total).astype(BF16)


def combine(parts, groups):
    tokens, wide = parts[0].shape
    hd = wide // (groups + 1)
    return pl.pallas_call(
        functools.partial(combine_kernel, groups),
        out_shape=jax.ShapeDtypeStruct((tokens, groups * hd), BF16),
        in_specs=[VMEM] * len(parts),
        out_specs=VMEM,
        compiler_params=pltpu.CompilerParams(vmem_limit_bytes=LIMIT),
        cost_estimate=cost(1e6, 1e6),
    )(*parts)


def project_kernel(nb, nw, *refs):
    ids = refs[0]
    blocks = refs[1 : 1 + nb]
    ws = refs[1 + nb : 1 + nb + nw]
    outs = refs[1 + nb + nw : -1]
    rows_s = refs[-1]
    tokens = blocks[0].shape[0]
    cols = ws[0].shape[1]
    for b in range(nb):
        rows_s[pl.ds(pl.multiple_of(ids[b] * tokens, tokens), tokens), :] = blocks[b][...]
    rows = rows_s[...]
    for w in range(nw):
        y = jnp.dot(rows, ws[w][...], preferred_element_type=F32).astype(BF16)
        for n, out in enumerate(outs):
            for half in range(2):
                lo = (2 * n + half) * tokens
                out[half, :, w * cols : (w + 1) * cols] = y[lo : lo + tokens]


def project(slots, blocks, ws, nx):
    tokens, width = blocks[0].shape
    nb, nw = len(blocks), len(ws)
    cols = ws[0].shape[1]
    out = jax.ShapeDtypeStruct((2, tokens, nw * cols), BF16)
    return pl.pallas_call(
        functools.partial(project_kernel, nb, nw),
        out_shape=[out] * nx,
        in_specs=[SMEM] + [VMEM] * (nb + nw),
        out_specs=[VMEM] * nx,
        scratch_shapes=[pltpu.VMEM((nb * tokens, width), BF16)],
        compiler_params=pltpu.CompilerParams(vmem_limit_bytes=LIMIT),
        cost_estimate=cost(2 * nb * tokens * width * nw * cols, 4e6),
    )(slots, *blocks, *ws)


def swap(array, axis):
    return lax.ppermute(array, axis, [(0, 1), (1, 0)])


def useful(plane, owner):
    return owner >= plane - 1 or plane == NZ - 1


def fetch(array, k, trim):
    pairs = [((z + k) % NZ, z) for z in range(NZ) if not trim or useful(z, (z + k) % NZ)]
    return lax.ppermute(array, "z", pairs)


def give(array, k):
    pairs = [(z, (z + k) % NZ) for z in range(NZ) if useful(z, (z + k) % NZ)]
    return lax.ppermute(array, "z", pairs)


def beside(array, flip):
    pairs = [
        ((z * 2 + y) * 2 + c, (((z + 2 * c - 1) % NZ) * 2 + (y ^ flip)) * 2 + c)
        for z in range(NZ)
        for y in range(2)
        for c in range(2)
        if not (z == NZ - 1 and c == 1)
    ]
    return lax.ppermute(array, ("z", "yh", "core"), pairs)


def per_device(
    queries, latent_keys, latent_values, key_basis, value_basis, out_weight, positions, key_segments
):
    z, yh, core = lax.axis_index("z"), lax.axis_index("yh"), lax.axis_index("core")
    yl, x = lax.axis_index("yl"), lax.axis_index("x")
    tokens, width = queries.shape
    hd = key_basis.shape[2]
    groups = width // hd
    span = latent_keys.shape[0]
    kv = rebuild(latent_keys, latent_values, key_basis, value_basis)
    lent, kv = lax.optimization_barrier((queries, kv))
    qs = [queries] + [fetch(lent, k, True) for k in SHIFTS[1:]]
    kv_y = swap(kv, "yh")
    kv_far, kv_far_y = beside(kv, 0), beside(kv, 1)

    def both_cores(array):
        return [array, swap(array, "core")]

    cut = span * 4 * NZ - jnp.sum(key_segments)
    qids = [4 * ((z + k) % NZ) + 2 * yh + core for k in SHIFTS]
    near, far = [], []
    for a in (0, 1):
        for b in (0, 1):
            place = 2 * (yh ^ a) + (core ^ b)
            near.append(4 * z + place)
            far.append(4 * ((z + 1 - 2 * (core ^ b)) % NZ) + place)
    ids_0 = jnp.stack(qids + near + [cut]).astype(jnp.int32)
    ids_1 = jnp.stack(qids + far + [cut]).astype(jnp.int32)
    pos = positions.reshape(-1, tokens)
    ids_0, ids_1, pos, kv_y, *qs = lax.optimization_barrier((ids_0, ids_1, pos, kv_y, *qs))
    state = flash(ids_0, pos, qs, both_cores(kv) + both_cores(kv_y), None, False)
    kv_far, kv_far_y, out_weight, *state = lax.optimization_barrier(
        (kv_far, kv_far_y, out_weight, *state)
    )
    w_y = swap(out_weight, "yh")
    parts = flash(ids_1, pos, qs, both_cores(kv_far) + both_cores(kv_far_y), state, True)
    w_y, *parts = lax.optimization_barrier((w_y, *parts))
    back = [parts[0]] + [give(part, k) for part, k in zip(parts[1:], SHIFTS[1:])]
    ws = [out_weight, swap(out_weight, "core"), w_y, swap(w_y, "core")]
    attended = combine(back, groups)

    up, down = fetch(attended, 1, False), fetch(attended, NZ - 1, False)
    up2, down2, far = [fetch(attended, k, False) for k in SHIFTS[1:]]
    blocks = [attended, up, down, up2, down2, far, fetch(up2, 1, False), fetch(down2, NZ - 1, False)]
    planes = [(z + k) % NZ for k in (0, 1, 7, 2, 6, 4, 3, 5)]
    slots = [2 * ((p % 4 - x) % 4) + ((p // 4) ^ yl) for p in planes]
    outs = project(jnp.stack(slots).astype(jnp.int32), blocks, ws, 4)

    def along_x(array, k):
        return lax.ppermute(array, "x", [(n, (n + k) % 4) for n in range(4)])

    summed = outs[0].astype(F32)
    for k in (1, 2, 3):
        summed = summed + along_x(outs[k], k).astype(F32)
    half = summed.shape[2] // 2

    def along_y(array, a, b):
        pairs = [(2 * m + n, 2 * (m ^ a) + (n ^ b)) for m in range(2) for n in range(2)]
        return lax.ppermute(array, ("yl", "yh"), pairs)

    sent = summed.astype(BF16)
    from_l = along_y(sent[1, :, :half], 1, 0)
    from_h = along_y(sent[0, :, half:], 0, 1)
    from_lh = along_y(sent[1, :, half:], 1, 1)
    mine = (summed[0, :, :half] + from_l.astype(F32)).astype(BF16)
    theirs = (from_h.astype(F32) + from_lh.astype(F32)).astype(BF16)
    both = jnp.stack([jnp.where(yh == 0, mine, theirs), jnp.where(yh == 0, theirs, mine)])
    cols = half // 2
    here = both[:, :, :cols]
    there = swap(both[:, :, cols:], "core")
    rows = jnp.stack([jnp.where(core == 0, here, there), jnp.where(core == 0, there, here)], axis=1)
    return rows.reshape(-1, cols)


def solution(mesh):
    fine = Mesh(mesh.devices.reshape(2, 4, NZ, 2, 2), ("yl", "x", "z", "yh", "core"))
    head, ctx = ("yl", "x"), ("z", "yh", "core")
    placed = (
        P(ctx, head),
        P(ctx, head),
        P(ctx, head),
        P(head, None, None),
        P(head, None, None),
        P(head, ctx),
        P(),
        P(),
    )
    return jax.shard_map(
        per_device, mesh=fine, in_specs=placed, out_specs=P(head, ctx), check_vma=False
    )
```

```python
import functools
import math

import jax
import jax.numpy as jnp
import numpy as np
from jax import lax
from jax.experimental import pallas as pl
from jax.experimental.pallas import tpu as pltpu
from jax.sharding import Mesh, PartitionSpec as P

NZ = 8
LAST = NZ - 1
NOWHERE = 1 << 16
FLOOR = -1e30
MASKED = -2e38
CLIMB = 40.0
F32 = jnp.float32
BF16 = jnp.bfloat16
VMEM = pl.BlockSpec(memory_space=pltpu.VMEM)
SMEM = pl.BlockSpec(memory_space=pltpu.SMEM)
ANY = pl.BlockSpec(memory_space=pl.ANY)
LIMIT = 24 * 1024 * 1024
FLASH_LIMIT = 40 * 1024 * 1024
REBUILD_LIMIT = 60 * 1024 * 1024
SHIFTS = (0, 2, 6, 4)


def cost(flops, moved):
    return pl.CostEstimate(flops=int(flops), bytes_accessed=int(moved), transcendentals=0)


def rebuild_kernel(lk_in, lv_in, bk_in, bv_in, kv_ref, lk_ref, lv_ref, bk_ref, bv_ref, sems):
    pairs = [(lk_in, lk_ref), (bk_in, bk_ref), (lv_in, lv_ref), (bv_in, bv_ref)]
    copies = [pltpu.make_async_copy(a, b, sems.at[n]) for n, (a, b) in enumerate(pairs)]
    for c in copies:
        c.start()
    for c in copies:
        c.wait()
    hd = bk_ref.shape[2]
    values = lax.dot_general(
        bv_ref[0], lv_ref[...], (((0,), (1,)), ((), ())), preferred_element_type=F32
    )
    kv_ref[:hd, :] = values.astype(BF16)
    for t in range(lk_ref.shape[0] // hd):
        part = slice(t * hd, (t + 1) * hd)
        keys = jnp.dot(lk_ref[part, :], bk_ref[0], preferred_element_type=F32)
        kv_ref[hd:, part] = keys.astype(BF16)


def rebuild(lk, lv, bk, bv):
    rows, hd = lk.shape[0], bk.shape[2]
    arrays = (lk, lv, bk, bv)
    return pl.pallas_call(
        rebuild_kernel,
        out_shape=jax.ShapeDtypeStruct((2 * hd, rows), BF16),
        in_specs=[ANY] * 4,
        out_specs=VMEM,
        scratch_shapes=[pltpu.VMEM(t.shape, t.dtype) for t in arrays]
        + [pltpu.SemaphoreType.DMA((4,))],
        compiler_params=pltpu.CompilerParams(vmem_limit_bytes=REBUILD_LIMIT),
        cost_estimate=cost(4 * rows * hd * hd, 8 * rows * hd),
    )(*arrays)


def flash_kernel(nq, nk, first, last, groups, rows, scale2, *refs):
    seg_in, pos_in = refs[0], refs[1]
    qs = refs[2 : 2 + nq]
    spare = refs[2 + nq]
    kvs = refs[3 + nq : 3 + nq + nk]
    at = 3 + nq + nk
    z, yh, core = lax.axis_index("z"), lax.axis_index("yh"), lax.axis_index("core")
    if not first:
        held = refs[at : at + 3 * nq]
        at += 3 * nq
    if last:
        outs = refs[at : at + nq]
        at += nq
    else:
        outs = refs[at : at + 3 * nq]
        at += 3 * nq
    flat_s, q_s, kv_s, pos_s, acc_t, begun, todo, m_s, l_s, acc_s, *rest = refs[at:]
    q_sem, kv_sem, st_sem, seg_ref, pos_ref, small_sem = rest
    hd = kvs[0].shape[0] // 2
    span = kvs[0].shape[1]
    tokens = qs[0].shape[0]
    kv_copies = [pltpu.make_async_copy(kvs[j], kv_s.at[j], kv_sem.at[j]) for j in range(nk)]
    q_copies = [pltpu.make_async_copy(qs[i], flat_s.at[i], q_sem.at[i]) for i in range(nq)]
    small = [
        pltpu.make_async_copy(seg_in, seg_ref, small_sem.at[0]),
        pltpu.make_async_copy(pos_in, pos_ref, small_sem.at[1]),
    ]
    for c in small + q_copies[:1] + q_copies[2:] + kv_copies:
        c.start()

    @pl.when(z == LAST - 1)
    def _():
        pltpu.make_async_copy(spare, flat_s.at[1], q_sem.at[1]).start()

    @pl.when(z != LAST - 1)
    def _():
        q_copies[1].start()

    if first:
        m_s[...] = jnp.full_like(m_s, FLOOR)
        l_s[...] = jnp.zeros_like(l_s)
        acc_s[...] = jnp.zeros_like(acc_s)
    else:
        held_copies = [
            pltpu.make_async_copy(r, (m_s, l_s, acc_s)[n % 3].at[n // 3], st_sem.at[n])
            for n, r in enumerate(held)
        ]
        for c in held_copies:
            c.start()
    for c in small:
        c.wait()
    cut = jnp.sum(jnp.where(seg_ref[...] == 0, 1.0, 0.0)).astype(jnp.int32)

    def query_block(i):
        plane = (z + SHIFTS[i]) & (NZ - 1)
        if i == 1:
            plane = jnp.where(z == LAST - 1, LAST, plane)
        return 4 * plane + 2 * yh + core

    def key_block(j):
        c = core ^ (j & 1)
        above = jnp.where(z == LAST - 2, NOWHERE, (z + 1) & (NZ - 1))
        below = jnp.where(z == LAST, 0, jnp.where(z < 2, NOWHERE, z - 1))
        beside = jnp.where(c == 0, above, below)
        if not first:
            return 4 * beside + 2 * (yh ^ 1) + c
        return 4 * jnp.where(j < 4, z, beside) + 2 * (yh ^ ((j >> 1) & 1)) + c

    for i in range(nq):
        block = query_block(i)
        per = pos_ref.shape[1] // tokens
        line = pos_ref[pl.ds(block // per, 1), :]
        row = line[:, :tokens]
        for n in range(1, per):
            row = jnp.where(block % per == n, line[:, n * tokens : (n + 1) * tokens], row)
        pos_s[i] = jnp.broadcast_to(jnp.concatenate([row] * groups, axis=1), (8, rows))
    for i in range(nq):
        q_copies[i].wait()
        for g in range(groups):
            q_s[i, g * tokens : (g + 1) * tokens, :] = flat_s[i, :, g * hd : (g + 1) * hd]
    if not first:
        for c in held_copies:
            c.wait()

    def scores_of(i, j, step):
        out = []
        for t in range(0, span, step):
            k = jnp.concatenate(
                [kv_s[j, hd:, u : u + hd] for u in range(t, t + step, hd)], axis=0
            )
            out.append(
                lax.dot_general(k, q_s[i], (((1,), (1,)), ((), ())), preferred_element_type=F32)
            )
        return out

    def safe_unit(i, j, ck):
        (s,) = scores_of(i, j, span)
        kpos = lax.broadcasted_iota(jnp.int32, (span, rows), 0) + ck * span
        pos = pos_s[i, :1, :]
        low = jnp.where(pos >= cut, cut, 0)
        s = jnp.where((kpos <= pos) & (kpos >= low), s, MASKED)
        s = s.reshape(span // 8, 8, rows)
        m_old = m_s[i]
        m_new = jnp.maximum(m_old, jnp.max(jnp.max(s, axis=0), axis=0, keepdims=True))
        fade = jnp.exp2((m_old - m_new) * scale2)
        p = jnp.exp2(s * scale2 - (m_new * scale2)[None])
        l_s[i] = l_s[i] * fade + jnp.sum(p, axis=0)
        acc_s[i] = acc_s[i] * fade[:1] + jnp.dot(
            kv_s[j, :hd, :], p.reshape(span, rows).astype(BF16), preferred_element_type=F32
        )
        m_s[i] = m_new

    def fast_unit(i, j):
        step = 2 * hd
        m_old = m_s[i]
        base = m_old * scale2
        top = m_old
        total = l_s[i]
        parts = []
        for s in scores_of(i, j, step):
            s = s.reshape(step // 8, 8, rows)
            top = jnp.maximum(top, jnp.max(s, axis=0))
            p = jnp.exp2(s * scale2 - base[None])
            total = total + jnp.sum(p, axis=0)
            parts.append(p.reshape(step, rows).astype(BF16))
        acc_t[...] = acc_s[i] + jnp.dot(
            kv_s[j, :hd, :], jnp.concatenate(parts, axis=0), preferred_element_type=F32
        )
        m_new = jnp.broadcast_to(jnp.max(top, axis=0, keepdims=True), (8, rows))
        climb = (m_new - m_old) * scale2
        fine = jnp.max(climb) < CLIMB

        @pl.when(fine)
        def _():
            fade = jnp.exp2(-climb)
            l_s[i] = total * fade
            acc_s[i] = acc_t[...] * fade[:1]
            m_s[i] = m_new

        return fine

    for i in range(nq):
        begun[i] = (jnp.max(m_s[i]) > 0.5 * FLOOR).astype(jnp.int32) if not first else jnp.int32(0)

    def one(n, carry):
        j = n // nq
        i = n % nq
        ck = key_block(j)
        cq = query_block(0)
        for n in range(1, nq):
            cq = jnp.where(i == n, query_block(n), cq)
        lent = (i == 1) & (z == LAST - 1)
        cq = jnp.where(lent & (j >= 4 if first else True), -1, cq)
        begin_k, end_k = ck * span, (ck + 1) * span
        begin_q, end_q = cq * span, (cq + 1) * span
        apart = (cut >= end_k) & (cut <= begin_q)
        whole = (ck < cq) & ((cut <= begin_k) | (cut >= end_q))
        some = (ck <= cq) & jnp.logical_not(apart)
        todo[0] = some.astype(jnp.int32)

        @pl.when(i == 0)
        def _():
            pltpu.make_async_copy(kv_s.at[j], kv_s.at[j], kv_sem.at[j]).wait()

        @pl.when(whole & (begun[i] == 0))
        def _():
            s = lax.dot_general(
                kv_s[j, hd:, :hd], q_s[i], (((1,), (1,)), ((), ())), preferred_element_type=F32
            )
            m_s[i] = jnp.broadcast_to(jnp.max(s, axis=0, keepdims=True), (8, rows))
            begun[i] = 1

        @pl.when(whole)
        def _():
            todo[0] = 1 - fast_unit(i, j).astype(jnp.int32)

        @pl.when(todo[0] > 0)
        def _():
            safe_unit(i, j, ck)
            begun[i] = 1

        return carry

    lax.fori_loop(0, nq * nk, one, 0)
    if not last:
        out_copies = [
            pltpu.make_async_copy((m_s, l_s, acc_s)[n % 3].at[n // 3], r, st_sem.at[n])
            for n, r in enumerate(outs)
        ]
        for c in out_copies:
            c.start()
        for c in out_copies:
            c.wait()
        return
    lane = lax.broadcasted_iota(jnp.int32, (tokens, hd), 1)
    for i in range(nq):
        total = jnp.sum(l_s[i], axis=0, keepdims=True)
        used = total > 0.0
        safe = jnp.where(used, total, 1.0)
        done = acc_s[i] * (1.0 / safe)
        level = jnp.where(used, m_s[i, :1, :] * scale2 + jnp.log2(safe), FLOOR)
        high = level.astype(BF16).astype(F32)
        mid = (level - high).astype(BF16).astype(F32)
        low = level - high - mid
        flag = jnp.where(used, 1.0, 0.0)
        stats = [high, mid, low, flag]
        table = jnp.concatenate(
            [v[:, g * tokens : (g + 1) * tokens] for v in stats for g in range(groups)]
            + [jnp.zeros((hd - 4 * groups, tokens), F32)],
            axis=0,
        )
        outs[i][:, groups * hd :] = table.T.astype(BF16)
        for g in range(groups):
            block = done[:, g * tokens : (g + 1) * tokens]
            outs[i][:, g * hd : (g + 1) * hd] = block.T.astype(BF16)


def flash(seg, pos, qs, spare, kvs, state, last):
    nq, nk = len(qs), len(kvs)
    tokens, width = qs[0].shape
    hd, span = kvs[0].shape[0] // 2, kvs[0].shape[1]
    groups = width // hd
    rows = groups * tokens
    scale2 = math.log2(math.e) * hd ** (-0.5)
    first = state is None
    state_types = [
        jax.ShapeDtypeStruct((8, rows), F32),
        jax.ShapeDtypeStruct((8, rows), F32),
        jax.ShapeDtypeStruct((hd, rows), F32),
    ]
    scratch = [
        pltpu.VMEM((nq, tokens, width), BF16),
        pltpu.VMEM((nq, rows, hd), BF16),
        pltpu.VMEM((nk, 2 * hd, span), BF16),
        pltpu.VMEM((nq, 8, rows), jnp.int32),
        pltpu.VMEM((hd, rows), F32),
        pltpu.SMEM((nq,), jnp.int32),
        pltpu.SMEM((1,), jnp.int32),
    ]
    scratch += [pltpu.VMEM((nq, *t.shape), t.dtype) for t in state_types]
    if last:
        outs = [jax.ShapeDtypeStruct((tokens, width + hd), BF16)] * nq
    else:
        outs = state_types * nq
    scratch += [
        pltpu.SemaphoreType.DMA((nq,)),
        pltpu.SemaphoreType.DMA((nk,)),
        pltpu.SemaphoreType.DMA((3 * nq,)),
        pltpu.VMEM(seg.shape, seg.dtype),
        pltpu.VMEM(pos.shape, pos.dtype),
        pltpu.SemaphoreType.DMA((2,)),
    ]
    return pl.pallas_call(
        functools.partial(flash_kernel, nq, nk, first, last, groups, rows, scale2),
        out_shape=outs,
        in_specs=[ANY] * (3 + nq + nk + (0 if first else 3 * nq)),
        out_specs=[VMEM if last else ANY] * len(outs),
        scratch_shapes=scratch,
        compiler_params=pltpu.CompilerParams(vmem_limit_bytes=FLASH_LIMIT),
        cost_estimate=cost(1e6, 1e5),
    )(seg, pos, *qs, spare, *kvs, *(() if first else state))


def combine_kernel(groups, *refs):
    parts, out = refs[:-1], refs[-1]
    tokens, width = out.shape
    hd = width // groups
    stats = [r[:, width:].astype(F32) for r in parts]
    for g in range(groups):
        levels = []
        for s in stats:
            level = (
                s[:, g : g + 1]
                + s[:, groups + g : groups + g + 1]
                + s[:, 2 * groups + g : 2 * groups + g + 1]
            )
            levels.append(jnp.where(s[:, 3 * groups + g : 3 * groups + g + 1] > 0.0, level, FLOOR))
        top = functools.reduce(jnp.maximum, levels)
        shares = [jnp.where(x > FLOOR, jnp.exp2(x - top), 0.0) for x in levels]
        total = functools.reduce(lambda a, b: a + b, shares)
        summed = 0.0
        for r, share in zip(parts, shares):
            summed = summed + r[:, g * hd : (g + 1) * hd].astype(F32) * share
        out[:, g * hd : (g + 1) * hd] = (summed / total).astype(BF16)


def combine(parts, groups):
    tokens, wide = parts[0].shape
    hd = wide // (groups + 1)
    return pl.pallas_call(
        functools.partial(combine_kernel, groups),
        out_shape=jax.ShapeDtypeStruct((tokens, groups * hd), BF16),
        in_specs=[VMEM] * len(parts),
        out_specs=VMEM,
        compiler_params=pltpu.CompilerParams(vmem_limit_bytes=LIMIT),
        cost_estimate=cost(1e6, 1e6),
    )(*parts)


def project_kernel(nb, nw, *refs):
    ids = refs[0]
    blocks = refs[1 : 1 + nb]
    ws = refs[1 + nb : 1 + nb + nw]
    outs = refs[1 + nb + nw : -1]
    rows_s = refs[-1]
    tokens = blocks[0].shape[0]
    cols = ws[0].shape[1]
    for b in range(nb):
        rows_s[pl.ds(pl.multiple_of(ids[b] * tokens, tokens), tokens), :] = blocks[b][...]
    rows = rows_s[...]
    for w in range(nw):
        y = jnp.dot(rows, ws[w][...], preferred_element_type=F32).astype(BF16)
        for n, out in enumerate(outs):
            for half in range(2):
                lo = (2 * n + half) * tokens
                out[half, :, w * cols : (w + 1) * cols] = y[lo : lo + tokens]


def project(slots, blocks, ws, nx):
    tokens, width = blocks[0].shape
    nb, nw = len(blocks), len(ws)
    cols = ws[0].shape[1]
    out = jax.ShapeDtypeStruct((2, tokens, nw * cols), BF16)
    return pl.pallas_call(
        functools.partial(project_kernel, nb, nw),
        out_shape=[out] * nx,
        in_specs=[SMEM] + [VMEM] * (nb + nw),
        out_specs=[VMEM] * nx,
        scratch_shapes=[pltpu.VMEM((nb * tokens, width), BF16)],
        compiler_params=pltpu.CompilerParams(vmem_limit_bytes=LIMIT),
        cost_estimate=cost(2 * nb * tokens * width * nw * cols, 4e6),
    )(slots, *blocks, *ws)


def swap(array, axis):
    return lax.ppermute(array, axis, [(0, 1), (1, 0)])


def useful(plane, owner):
    return owner >= plane - 1 or plane == NZ - 1


def fetch(array, k, trim):
    pairs = [((z + k) % NZ, z) for z in range(NZ) if not trim or useful(z, (z + k) % NZ)]
    return lax.ppermute(array, "z", pairs)


def give(array, k):
    pairs = [(z, (z + k) % NZ) for z in range(NZ) if useful(z, (z + k) % NZ)]
    return lax.ppermute(array, "z", pairs)


def lender(z, c):
    if c == 0:
        return None if z == LAST - 2 else (z + 1) % NZ
    return {0: None, 1: None, LAST: 0}.get(z, z - 1)


def beside(array):
    pairs = [
        ((lender(z, c) * 2 + y) * 2 + c, (z * 2 + y) * 2 + c)
        for z in range(NZ)
        for y in range(2)
        for c in range(2)
        if lender(z, c) is not None
    ]
    return lax.ppermute(array, ("z", "yh", "core"), pairs)


def per_device(
    queries, latent_keys, latent_values, key_basis, value_basis, out_weight, positions, key_segments
):
    z, yh, core = lax.axis_index("z"), lax.axis_index("yh"), lax.axis_index("core")
    yl, x = lax.axis_index("yl"), lax.axis_index("x")
    tokens, width = queries.shape
    hd = key_basis.shape[2]
    groups = width // hd
    span = latent_keys.shape[0]
    kv = rebuild(latent_keys, latent_values, key_basis, value_basis)
    lent, kv = lax.optimization_barrier((queries, kv))
    q_far = fetch(lent, 4, True)
    q_down = fetch(lent, 6, True)
    spare = lax.ppermute(lent, "z", [(LAST, LAST - 1)])
    qs = [queries, fetch(lent, 2, True), q_down, q_far]
    kv_y = swap(kv, "yh")
    kv_far = beside(kv)

    def both_cores(array):
        return [array, swap(array, "core")]

    seg, pos = key_segments.reshape(-1, 128), positions.reshape(-1, 128)
    kv, kv_y, kv_far, spare, *qs = lax.optimization_barrier((kv, kv_y, kv_far, spare, *qs))
    kv_far_y = swap(kv_far, "yh")
    kvs = both_cores(kv) + both_cores(kv_y) + both_cores(kv_far)
    state = flash(seg, pos, qs, spare, kvs, None, False)
    kv_far_y, out_weight, *state = lax.optimization_barrier((kv_far_y, out_weight, *state))
    w_y = swap(out_weight, "yh")
    parts = flash(seg, pos, qs, spare, both_cores(kv_far_y), state, True)
    back = [parts[0]] + [give(parts[n], SHIFTS[n]) for n in (3, 1, 2)]
    back += [lax.ppermute(parts[1], "z", [(LAST - 1, LAST)])]
    attended = combine(back, groups)
    w_y, attended = lax.optimization_barrier((w_y, attended))
    ws = [out_weight, swap(out_weight, "core"), w_y, swap(w_y, "core")]

    up, down = fetch(attended, 1, False), fetch(attended, NZ - 1, False)
    up2, down2, far = [fetch(attended, k, False) for k in SHIFTS[1:]]
    blocks = [attended, up, down, up2, down2, far, fetch(up2, 1, False), fetch(down2, NZ - 1, False)]
    planes = [(z + k) % NZ for k in (0, 1, 7, 2, 6, 4, 3, 5)]
    slots = [2 * ((p % 4 - x) % 4) + ((p // 4) ^ yl) for p in planes]
    outs = project(jnp.stack(slots).astype(jnp.int32), blocks, ws, 4)

    def along_x(array, k):
        return lax.ppermute(array, "x", [(n, (n + k) % 4) for n in range(4)])

    summed = outs[0].astype(F32)
    for k in (1, 2, 3):
        summed = summed + along_x(outs[k], k).astype(F32)
    half = summed.shape[2] // 2

    def along_y(array, a, b):
        pairs = [(2 * m + n, 2 * (m ^ a) + (n ^ b)) for m in range(2) for n in range(2)]
        return lax.ppermute(array, ("yl", "yh"), pairs)

    sent = summed.astype(BF16)
    from_l = along_y(sent[1, :, :half], 1, 0)
    from_h = along_y(sent[0, :, half:], 0, 1)
    from_lh = along_y(sent[1, :, half:], 1, 1)
    mine = (summed[0, :, :half] + from_l.astype(F32)).astype(BF16)
    theirs = (from_h.astype(F32) + from_lh.astype(F32)).astype(BF16)
    both = jnp.stack([jnp.where(yh == 0, mine, theirs), jnp.where(yh == 0, theirs, mine)])
    cols = half // 2
    here = both[:, :, :cols]
    there = swap(both[:, :, cols:], "core")
    rows = jnp.stack([jnp.where(core == 0, here, there), jnp.where(core == 0, there, here)], axis=1)
    return rows.reshape(-1, cols)


def solution(mesh):
    fine = Mesh(mesh.devices.reshape(2, 4, NZ, 2, 2), ("yl", "x", "z", "yh", "core"))
    head, ctx = ("yl", "x"), ("z", "yh", "core")
    placed = (
        P(ctx, head),
        P(ctx, head),
        P(ctx, head),
        P(head, None, None),
        P(head, None, None),
        P(head, ctx),
        P(),
        P(),
    )
    return jax.shard_map(
        per_device, mesh=fine, in_specs=placed, out_specs=P(head, ctx), check_vma=False
    )
```

```python
import functools
import math

import jax
import jax.numpy as jnp
import numpy as np
from jax import lax
from jax.experimental import pallas as pl
from jax.experimental.pallas import tpu as pltpu
from jax.sharding import Mesh, PartitionSpec as P

NZ = 8
LAST = NZ - 1
NOWHERE = 1 << 16
FLOOR = -1e30
MASKED = -2e38
CLIMB = 40.0
F32 = jnp.float32
BF16 = jnp.bfloat16
VMEM = pl.BlockSpec(memory_space=pltpu.VMEM)
SMEM = pl.BlockSpec(memory_space=pltpu.SMEM)
ANY = pl.BlockSpec(memory_space=pl.ANY)
LIMIT = 24 * 1024 * 1024
FLASH_LIMIT = 40 * 1024 * 1024
REBUILD_LIMIT = 60 * 1024 * 1024
SHIFTS = (0, 2, 6, 4)


def cost(flops, moved):
    return pl.CostEstimate(flops=int(flops), bytes_accessed=int(moved), transcendentals=0)


def rebuild_kernel(lk_in, lv_in, bk_in, bv_in, kv_ref, lk_ref, lv_ref, bk_ref, bv_ref, sems):
    pairs = [(lk_in, lk_ref), (bk_in, bk_ref), (lv_in, lv_ref), (bv_in, bv_ref)]
    copies = [pltpu.make_async_copy(a, b, sems.at[n]) for n, (a, b) in enumerate(pairs)]
    for c in copies:
        c.start()
    for c in copies:
        c.wait()
    hd = bk_ref.shape[2]
    values = lax.dot_general(
        bv_ref[0], lv_ref[...], (((0,), (1,)), ((), ())), preferred_element_type=F32
    )
    kv_ref[:hd, :] = values.astype(BF16)
    for t in range(lk_ref.shape[0] // hd):
        part = slice(t * hd, (t + 1) * hd)
        keys = jnp.dot(lk_ref[part, :], bk_ref[0], preferred_element_type=F32)
        kv_ref[hd:, part] = keys.astype(BF16)


def rebuild(lk, lv, bk, bv):
    rows, hd = lk.shape[0], bk.shape[2]
    arrays = (lk, lv, bk, bv)
    return pl.pallas_call(
        rebuild_kernel,
        out_shape=jax.ShapeDtypeStruct((2 * hd, rows), BF16),
        in_specs=[ANY] * 4,
        out_specs=VMEM,
        scratch_shapes=[pltpu.VMEM(t.shape, t.dtype) for t in arrays]
        + [pltpu.SemaphoreType.DMA((4,))],
        compiler_params=pltpu.CompilerParams(vmem_limit_bytes=REBUILD_LIMIT),
        cost_estimate=cost(4 * rows * hd * hd, 8 * rows * hd),
    )(*arrays)


def flash_kernel(nq, nk, first, last, groups, rows, scale2, *refs):
    seg_in, pos_in = refs[0], refs[1]
    qs = refs[2 : 2 + nq]
    spare = refs[2 + nq]
    kvs = refs[3 + nq : 3 + nq + nk]
    at = 3 + nq + nk
    z, yh, core = lax.axis_index("z"), lax.axis_index("yh"), lax.axis_index("core")
    if not first:
        held = refs[at : at + 3 * nq]
        at += 3 * nq
    if last:
        outs = refs[at : at + nq]
        at += nq
    else:
        outs = refs[at : at + 3 * nq]
        at += 3 * nq
    flat_s, q_s, kv_s, pos_s, acc_t, begun, m_s, l_s, acc_s, *rest = refs[at:]
    q_sem, kv_sem, st_sem, seg_ref, pos_ref, small_sem = rest
    hd = kvs[0].shape[0] // 2
    span = kvs[0].shape[1]
    tokens = qs[0].shape[0]
    kv_copies = [pltpu.make_async_copy(kvs[j], kv_s.at[j], kv_sem.at[j]) for j in range(nk)]
    q_copies = [pltpu.make_async_copy(qs[i], flat_s.at[i], q_sem.at[i]) for i in range(nq)]
    small = [
        pltpu.make_async_copy(seg_in, seg_ref, small_sem.at[0]),
        pltpu.make_async_copy(pos_in, pos_ref, small_sem.at[1]),
    ]
    for c in small + q_copies[:1] + q_copies[2:] + kv_copies:
        c.start()

    @pl.when(z == LAST - 1)
    def _():
        pltpu.make_async_copy(spare, flat_s.at[1], q_sem.at[1]).start()

    @pl.when(z != LAST - 1)
    def _():
        q_copies[1].start()

    if first:
        m_s[...] = jnp.full_like(m_s, FLOOR)
        l_s[...] = jnp.zeros_like(l_s)
        acc_s[...] = jnp.zeros_like(acc_s)
    else:
        held_copies = [
            pltpu.make_async_copy(r, (m_s, l_s, acc_s)[n % 3].at[n // 3], st_sem.at[n])
            for n, r in enumerate(held)
        ]
        for c in held_copies:
            c.start()
    for c in small:
        c.wait()
    cut = jnp.sum(jnp.where(seg_ref[...] == 0, 1.0, 0.0)).astype(jnp.int32)

    def query_block(i):
        plane = (z + SHIFTS[i]) & (NZ - 1)
        if i == 1:
            plane = jnp.where(z == LAST - 1, LAST, plane)
        return 4 * plane + 2 * yh + core

    def key_block(j):
        c = core ^ (j & 1)
        above = jnp.where(z == LAST - 2, NOWHERE, (z + 1) & (NZ - 1))
        below = jnp.where(z == LAST, 0, jnp.where(z < 2, NOWHERE, z - 1))
        beside = jnp.where(c == 0, above, below)
        if not first:
            return 4 * beside + 2 * (yh ^ 1) + c
        return 4 * jnp.where(j < 4, z, beside) + 2 * (yh ^ ((j >> 1) & 1)) + c

    for i in range(nq):
        block = query_block(i)
        per = pos_ref.shape[1] // tokens
        line = pos_ref[pl.ds(block // per, 1), :]
        row = line[:, :tokens]
        for n in range(1, per):
            row = jnp.where(block % per == n, line[:, n * tokens : (n + 1) * tokens], row)
        pos_s[i] = jnp.broadcast_to(jnp.concatenate([row] * groups, axis=1), (8, rows))
    for i in range(nq):
        q_copies[i].wait()
        for g in range(groups):
            q_s[i, g * tokens : (g + 1) * tokens, :] = flat_s[i, :, g * hd : (g + 1) * hd]
    if not first:
        for c in held_copies:
            c.wait()

    def scores_of(i, j, step):
        out = []
        for t in range(0, span, step):
            k = jnp.concatenate(
                [kv_s[j, hd:, u : u + hd] for u in range(t, t + step, hd)], axis=0
            )
            out.append(
                lax.dot_general(k, q_s[i], (((1,), (1,)), ((), ())), preferred_element_type=F32)
            )
        return out

    def safe_unit(i, j, ck):
        (s,) = scores_of(i, j, span)
        kpos = lax.broadcasted_iota(jnp.int32, (span, rows), 0) + ck * span
        pos = pos_s[i, :1, :]
        low = jnp.where(pos >= cut, cut, 0)
        s = jnp.where((kpos <= pos) & (kpos >= low), s, MASKED)
        s = s.reshape(span // 8, 8, rows)
        m_old = m_s[i]
        m_new = jnp.maximum(m_old, jnp.max(jnp.max(s, axis=0), axis=0, keepdims=True))
        fade = jnp.exp2((m_old - m_new) * scale2)
        p = jnp.exp2(s * scale2 - (m_new * scale2)[None])
        l_s[i] = l_s[i] * fade + jnp.sum(p, axis=0)
        acc_s[i] = acc_s[i] * fade[:1] + jnp.dot(
            kv_s[j, :hd, :], p.reshape(span, rows).astype(BF16), preferred_element_type=F32
        )
        m_s[i] = m_new

    def fast_unit(i, j):
        step = 2 * hd
        m_old = m_s[i]
        base = m_old * scale2
        top = m_old
        total = l_s[i]
        parts = []
        for s in scores_of(i, j, step):
            s = s.reshape(step // 8, 8, rows)
            top = jnp.maximum(top, jnp.max(s, axis=0))
            p = jnp.exp2(s * scale2 - base[None])
            total = total + jnp.sum(p, axis=0)
            parts.append(p.reshape(step, rows).astype(BF16))
        acc_t[...] = acc_s[i] + jnp.dot(
            kv_s[j, :hd, :], jnp.concatenate(parts, axis=0), preferred_element_type=F32
        )
        m_new = jnp.broadcast_to(jnp.max(top, axis=0, keepdims=True), (8, rows))
        climb = (m_new - m_old) * scale2
        fine = jnp.max(climb) < CLIMB

        @pl.when(fine)
        def _():
            fade = jnp.exp2(-climb)
            l_s[i] = total * fade
            acc_s[i] = acc_t[...] * fade[:1]
            m_s[i] = m_new

        return fine

    for i in range(nq):
        begun[i] = (jnp.max(m_s[i]) > 0.5 * FLOOR).astype(jnp.int32) if not first else jnp.int32(0)

    asked = [query_block(n) for n in range(nq)]

    def one(n, carry):
        j = lax.div(n, jnp.int32(nq))
        i = lax.rem(n, jnp.int32(nq))
        ck = key_block(j)
        cq = asked[0]
        for m in range(1, nq):
            cq = jnp.where(i == m, asked[m], cq)
        lent = (i == 1) & (z == LAST - 1)
        cq = jnp.where(lent & (j >= 4 if first else True), -1, cq)
        begin_k, end_k = ck * span, (ck + 1) * span
        begin_q, end_q = cq * span, (cq + 1) * span
        apart = (cut >= end_k) & (cut <= begin_q)
        whole = (ck < cq) & ((cut <= begin_k) | (cut >= end_q))
        some = (ck <= cq) & jnp.logical_not(apart)

        @pl.when(i == 0)
        def _():
            pltpu.make_async_copy(kv_s.at[j], kv_s.at[j], kv_sem.at[j]).wait()

        @pl.when(whole & (begun[i] == 0))
        def _():
            s = lax.dot_general(
                kv_s[j, hd:, :hd], q_s[i], (((1,), (1,)), ((), ())), preferred_element_type=F32
            )
            m_s[i] = jnp.broadcast_to(jnp.max(s, axis=0, keepdims=True), (8, rows))
            begun[i] = 1

        left = lax.cond(
            whole,
            lambda: 1 - fast_unit(i, j).astype(jnp.int32),
            lambda: some.astype(jnp.int32),
        )

        @pl.when(left > 0)
        def _():
            safe_unit(i, j, ck)
            begun[i] = 1

        return carry

    lax.fori_loop(0, nq * nk, one, 0)
    if not last:
        out_copies = [
            pltpu.make_async_copy((m_s, l_s, acc_s)[n % 3].at[n // 3], r, st_sem.at[n])
            for n, r in enumerate(outs)
        ]
        for c in out_copies:
            c.start()
        for c in out_copies:
            c.wait()
        return
    lane = lax.broadcasted_iota(jnp.int32, (tokens, hd), 1)
    for i in range(nq):
        total = jnp.sum(l_s[i], axis=0, keepdims=True)
        used = total > 0.0
        safe = jnp.where(used, total, 1.0)
        done = acc_s[i] * (1.0 / safe)
        level = jnp.where(used, m_s[i, :1, :] * scale2 + jnp.log2(safe), FLOOR)
        high = level.astype(BF16).astype(F32)
        mid = (level - high).astype(BF16).astype(F32)
        low = level - high - mid
        flag = jnp.where(used, 1.0, 0.0)
        stats = [high, mid, low, flag]
        table = jnp.concatenate(
            [v[:, g * tokens : (g + 1) * tokens] for v in stats for g in range(groups)]
            + [jnp.zeros((hd - 4 * groups, tokens), F32)],
            axis=0,
        )
        outs[i][:, groups * hd :] = table.T.astype(BF16)
        for g in range(groups):
            block = done[:, g * tokens : (g + 1) * tokens]
            outs[i][:, g * hd : (g + 1) * hd] = block.T.astype(BF16)


def flash(seg, pos, qs, spare, kvs, state, last):
    nq, nk = len(qs), len(kvs)
    tokens, width = qs[0].shape
    hd, span = kvs[0].shape[0] // 2, kvs[0].shape[1]
    groups = width // hd
    rows = groups * tokens
    scale2 = math.log2(math.e) * hd ** (-0.5)
    first = state is None
    state_types = [
        jax.ShapeDtypeStruct((8, rows), F32),
        jax.ShapeDtypeStruct((8, rows), F32),
        jax.ShapeDtypeStruct((hd, rows), F32),
    ]
    scratch = [
        pltpu.VMEM((nq, tokens, width), BF16),
        pltpu.VMEM((nq, rows, hd), BF16),
        pltpu.VMEM((nk, 2 * hd, span), BF16),
        pltpu.VMEM((nq, 8, rows), jnp.int32),
        pltpu.VMEM((hd, rows), F32),
        pltpu.SMEM((nq,), jnp.int32),
    ]
    scratch += [pltpu.VMEM((nq, *t.shape), t.dtype) for t in state_types]
    if last:
        outs = [jax.ShapeDtypeStruct((tokens, width + hd), BF16)] * nq
    else:
        outs = state_types * nq
    scratch += [
        pltpu.SemaphoreType.DMA((nq,)),
        pltpu.SemaphoreType.DMA((nk,)),
        pltpu.SemaphoreType.DMA((3 * nq,)),
        pltpu.VMEM(seg.shape, seg.dtype),
        pltpu.VMEM(pos.shape, pos.dtype),
        pltpu.SemaphoreType.DMA((2,)),
    ]
    return pl.pallas_call(
        functools.partial(flash_kernel, nq, nk, first, last, groups, rows, scale2),
        out_shape=outs,
        in_specs=[ANY] * (3 + nq + nk + (0 if first else 3 * nq)),
        out_specs=[VMEM if last else ANY] * len(outs),
        scratch_shapes=scratch,
        compiler_params=pltpu.CompilerParams(vmem_limit_bytes=FLASH_LIMIT),
        cost_estimate=cost(1e6, 1e5),
    )(seg, pos, *qs, spare, *kvs, *(() if first else state))


def combine_kernel(groups, *refs):
    parts, out = refs[:-1], refs[-1]
    tokens, width = out.shape
    hd = width // groups
    stats = [r[:, width:].astype(F32) for r in parts]
    for g in range(groups):
        levels = []
        for s in stats:
            level = (
                s[:, g : g + 1]
                + s[:, groups + g : groups + g + 1]
                + s[:, 2 * groups + g : 2 * groups + g + 1]
            )
            levels.append(jnp.where(s[:, 3 * groups + g : 3 * groups + g + 1] > 0.0, level, FLOOR))
        top = functools.reduce(jnp.maximum, levels)
        shares = [jnp.where(x > FLOOR, jnp.exp2(x - top), 0.0) for x in levels]
        total = functools.reduce(lambda a, b: a + b, shares)
        summed = 0.0
        for r, share in zip(parts, shares):
            summed = summed + r[:, g * hd : (g + 1) * hd].astype(F32) * share
        out[:, g * hd : (g + 1) * hd] = (summed / total).astype(BF16)


def combine(parts, groups):
    tokens, wide = parts[0].shape
    hd = wide // (groups + 1)
    return pl.pallas_call(
        functools.partial(combine_kernel, groups),
        out_shape=jax.ShapeDtypeStruct((tokens, groups * hd), BF16),
        in_specs=[VMEM] * len(parts),
        out_specs=VMEM,
        compiler_params=pltpu.CompilerParams(vmem_limit_bytes=LIMIT),
        cost_estimate=cost(1e6, 1e6),
    )(*parts)


def project_kernel(nb, nw, *refs):
    ids = refs[0]
    blocks = refs[1 : 1 + nb]
    ws = refs[1 + nb : 1 + nb + nw]
    outs = refs[1 + nb + nw : -1]
    rows_s = refs[-1]
    tokens = blocks[0].shape[0]
    cols = ws[0].shape[1]
    for b in range(nb):
        rows_s[pl.ds(pl.multiple_of(ids[b] * tokens, tokens), tokens), :] = blocks[b][...]
    rows = rows_s[...]
    for w in range(nw):
        y = jnp.dot(rows, ws[w][...], preferred_element_type=F32).astype(BF16)
        for n, out in enumerate(outs):
            for half in range(2):
                lo = (2 * n + half) * tokens
                out[half, :, w * cols : (w + 1) * cols] = y[lo : lo + tokens]


def project(slots, blocks, ws, nx):
    tokens, width = blocks[0].shape
    nb, nw = len(blocks), len(ws)
    cols = ws[0].shape[1]
    out = jax.ShapeDtypeStruct((2, tokens, nw * cols), BF16)
    return pl.pallas_call(
        functools.partial(project_kernel, nb, nw),
        out_shape=[out] * nx,
        in_specs=[SMEM] + [VMEM] * (nb + nw),
        out_specs=[VMEM] * nx,
        scratch_shapes=[pltpu.VMEM((nb * tokens, width), BF16)],
        compiler_params=pltpu.CompilerParams(vmem_limit_bytes=LIMIT),
        cost_estimate=cost(2 * nb * tokens * width * nw * cols, 4e6),
    )(slots, *blocks, *ws)


def swap(array, axis):
    return lax.ppermute(array, axis, [(0, 1), (1, 0)])


def useful(plane, owner):
    return owner >= plane - 1 or plane == NZ - 1


def fetch(array, k, trim):
    pairs = [((z + k) % NZ, z) for z in range(NZ) if not trim or useful(z, (z + k) % NZ)]
    return lax.ppermute(array, "z", pairs)


def give(array, k):
    pairs = [(z, (z + k) % NZ) for z in range(NZ) if useful(z, (z + k) % NZ)]
    return lax.ppermute(array, "z", pairs)


def lender(z, c):
    if c == 0:
        return None if z == LAST - 2 else (z + 1) % NZ
    return {0: None, 1: None, LAST: 0}.get(z, z - 1)


def beside(array):
    pairs = [
        ((lender(z, c) * 2 + y) * 2 + c, (z * 2 + y) * 2 + c)
        for z in range(NZ)
        for y in range(2)
        for c in range(2)
        if lender(z, c) is not None
    ]
    return lax.ppermute(array, ("z", "yh", "core"), pairs)


def per_device(
    queries, latent_keys, latent_values, key_basis, value_basis, out_weight, positions, key_segments
):
    z, yh, core = lax.axis_index("z"), lax.axis_index("yh"), lax.axis_index("core")
    yl, x = lax.axis_index("yl"), lax.axis_index("x")
    tokens, width = queries.shape
    hd = key_basis.shape[2]
    groups = width // hd
    span = latent_keys.shape[0]
    kv = rebuild(latent_keys, latent_values, key_basis, value_basis)
    lent = queries
    q_far = fetch(lent, 4, True)
    q_down = fetch(lent, 6, True)
    spare = lax.ppermute(lent, "z", [(LAST, LAST - 1)])
    qs = [queries, fetch(lent, 2, True), q_down, q_far]
    kv_y = swap(kv, "yh")
    kv_far = beside(kv)

    def both_cores(array):
        return [array, swap(array, "core")]

    seg, pos = key_segments.reshape(-1, 128), positions.reshape(-1, 128)
    q_up, q_down, q_far = qs[1:]
    q_far, q_up, q_down, kv, kv_y, kv_far, spare = lax.optimization_barrier(
        (q_far, q_up, q_down, kv, kv_y, kv_far, spare)
    )
    qs = [queries, q_up, q_down, q_far]
    kv_far_y = swap(kv_far, "yh")
    kvs = both_cores(kv) + both_cores(kv_y) + both_cores(kv_far)
    state = flash(seg, pos, qs, spare, kvs, None, False)
    kv_far_y, out_weight, *state = lax.optimization_barrier((kv_far_y, out_weight, *state))
    w_y = swap(out_weight, "yh")
    parts = flash(seg, pos, qs, spare, both_cores(kv_far_y), state, True)
    back = [parts[0]] + [give(parts[n], SHIFTS[n]) for n in (3, 1, 2)]
    back += [lax.ppermute(parts[1], "z", [(LAST - 1, LAST)])]
    attended = combine(back, groups)
    w_y, attended = lax.optimization_barrier((w_y, attended))
    ws = [out_weight, swap(out_weight, "core"), w_y, swap(w_y, "core")]

    up, down = fetch(attended, 1, False), fetch(attended, NZ - 1, False)
    up2, down2, far = [fetch(attended, k, False) for k in SHIFTS[1:]]
    blocks = [attended, up, down, up2, down2, far, fetch(up2, 1, False), fetch(down2, NZ - 1, False)]
    planes = [(z + k) % NZ for k in (0, 1, 7, 2, 6, 4, 3, 5)]
    slots = [2 * ((p % 4 - x) % 4) + ((p // 4) ^ yl) for p in planes]
    outs = project(jnp.stack(slots).astype(jnp.int32), blocks, ws, 4)

    def along_x(array, k):
        return lax.ppermute(array, "x", [(n, (n + k) % 4) for n in range(4)])

    summed = outs[0].astype(F32)
    for k in (1, 2, 3):
        summed = summed + along_x(outs[k], k).astype(F32)
    half = summed.shape[2] // 2

    def along_y(array, a, b):
        pairs = [(2 * m + n, 2 * (m ^ a) + (n ^ b)) for m in range(2) for n in range(2)]
        return lax.ppermute(array, ("yl", "yh"), pairs)

    sent = summed.astype(BF16)
    from_l = along_y(sent[1, :, :half], 1, 0)
    from_h = along_y(sent[0, :, half:], 0, 1)
    from_lh = along_y(sent[1, :, half:], 1, 1)
    mine = (summed[0, :, :half] + from_l.astype(F32)).astype(BF16)
    theirs = (from_h.astype(F32) + from_lh.astype(F32)).astype(BF16)
    both = jnp.stack([jnp.where(yh == 0, mine, theirs), jnp.where(yh == 0, theirs, mine)])
    cols = half // 2
    here = both[:, :, :cols]
    there = swap(both[:, :, cols:], "core")
    rows = jnp.stack([jnp.where(core == 0, here, there), jnp.where(core == 0, there, here)], axis=1)
    return rows.reshape(-1, cols)


def solution(mesh):
    fine = Mesh(mesh.devices.reshape(2, 4, NZ, 2, 2), ("yl", "x", "z", "yh", "core"))
    head, ctx = ("yl", "x"), ("z", "yh", "core")
    placed = (
        P(ctx, head),
        P(ctx, head),
        P(ctx, head),
        P(head, None, None),
        P(head, None, None),
        P(head, ctx),
        P(),
        P(),
    )
    return jax.shard_map(
        per_device, mesh=fine, in_specs=placed, out_specs=P(head, ctx), check_vma=False
    )
```

```python
import functools
import math

import jax
import jax.numpy as jnp
import numpy as np
from jax import lax
from jax.experimental import pallas as pl
from jax.experimental.pallas import tpu as pltpu
from jax.sharding import Mesh, PartitionSpec as P

NZ = 8
LAST = NZ - 1
NOWHERE = 1 << 16
FLOOR = -1e30
MASKED = -2e38
CLIMB = 40.0
F32 = jnp.float32
BF16 = jnp.bfloat16
VMEM = pl.BlockSpec(memory_space=pltpu.VMEM)
SMEM = pl.BlockSpec(memory_space=pltpu.SMEM)
ANY = pl.BlockSpec(memory_space=pl.ANY)
LIMIT = 24 * 1024 * 1024
FLASH_LIMIT = 40 * 1024 * 1024
REBUILD_LIMIT = 60 * 1024 * 1024
SHIFTS = (0, 2, 6, 4)


def cost(flops, moved):
    return pl.CostEstimate(flops=int(flops), bytes_accessed=int(moved), transcendentals=0)


def rebuild_kernel(lk_in, lv_in, bk_in, bv_in, kv_ref, lk_ref, lv_ref, bk_ref, bv_ref, sems):
    pairs = [(lk_in, lk_ref), (bk_in, bk_ref), (lv_in, lv_ref), (bv_in, bv_ref)]
    copies = [pltpu.make_async_copy(a, b, sems.at[n]) for n, (a, b) in enumerate(pairs)]
    for c in copies:
        c.start()
    for c in copies:
        c.wait()
    hd = bk_ref.shape[2]
    values = lax.dot_general(
        bv_ref[0], lv_ref[...], (((0,), (1,)), ((), ())), preferred_element_type=F32
    )
    kv_ref[:hd, :] = values.astype(BF16)
    for t in range(lk_ref.shape[0] // hd):
        part = slice(t * hd, (t + 1) * hd)
        keys = jnp.dot(lk_ref[part, :], bk_ref[0], preferred_element_type=F32)
        kv_ref[hd:, part] = keys.astype(BF16)


def rebuild(lk, lv, bk, bv):
    rows, hd = lk.shape[0], bk.shape[2]
    arrays = (lk, lv, bk, bv)
    return pl.pallas_call(
        rebuild_kernel,
        out_shape=jax.ShapeDtypeStruct((2 * hd, rows), BF16),
        in_specs=[ANY] * 4,
        out_specs=VMEM,
        scratch_shapes=[pltpu.VMEM(t.shape, t.dtype) for t in arrays]
        + [pltpu.SemaphoreType.DMA((4,))],
        compiler_params=pltpu.CompilerParams(vmem_limit_bytes=REBUILD_LIMIT),
        cost_estimate=cost(4 * rows * hd * hd, 8 * rows * hd),
    )(*arrays)


def flash_kernel(nq, nk, first, last, groups, rows, scale2, *refs):
    seg_in, pos_in = refs[0], refs[1]
    qs = refs[2 : 2 + nq]
    spare = refs[2 + nq]
    kvs = refs[3 + nq : 3 + nq + nk]
    at = 3 + nq + nk
    z, yh, core = lax.axis_index("z"), lax.axis_index("yh"), lax.axis_index("core")
    if not first:
        held = refs[at : at + 3 * nq]
        at += 3 * nq
    if last:
        outs = refs[at : at + nq]
        at += nq
    else:
        outs = refs[at : at + 3 * nq]
        at += 3 * nq
    flat_s, q_s, kv_s, pos_s, acc_t, begun, todo, m_s, l_s, acc_s, *rest = refs[at:]
    q_sem, kv_sem, st_sem, seg_ref, pos_ref, small_sem = rest
    hd = kvs[0].shape[0] // 2
    span = kvs[0].shape[1]
    tokens = qs[0].shape[0]
    kv_copies = [pltpu.make_async_copy(kvs[j], kv_s.at[j], kv_sem.at[j]) for j in range(nk)]
    q_copies = [pltpu.make_async_copy(qs[i], flat_s.at[i], q_sem.at[i]) for i in range(nq)]
    small = [
        pltpu.make_async_copy(seg_in, seg_ref, small_sem.at[0]),
        pltpu.make_async_copy(pos_in, pos_ref, small_sem.at[1]),
    ]
    for c in small + q_copies[:1] + q_copies[2:] + kv_copies:
        c.start()

    @pl.when(z == LAST - 1)
    def _():
        pltpu.make_async_copy(spare, flat_s.at[1], q_sem.at[1]).start()

    @pl.when(z != LAST - 1)
    def _():
        q_copies[1].start()

    if first:
        m_s[...] = jnp.full_like(m_s, FLOOR)
        l_s[...] = jnp.zeros_like(l_s)
        acc_s[...] = jnp.zeros_like(acc_s)
    else:
        held_copies = [
            pltpu.make_async_copy(r, (m_s, l_s, acc_s)[n % 3].at[n // 3], st_sem.at[n])
            for n, r in enumerate(held)
        ]
        for c in held_copies:
            c.start()
    for c in small:
        c.wait()
    cut = jnp.sum(jnp.where(seg_ref[...] == 0, 1.0, 0.0)).astype(jnp.int32)

    def query_block(i):
        plane = (z + SHIFTS[i]) & (NZ - 1)
        if i == 1:
            plane = jnp.where(z == LAST - 1, LAST, plane)
        return 4 * plane + 2 * yh + core

    def key_block(j):
        c = core ^ (j & 1)
        above = jnp.where(z == LAST - 2, NOWHERE, (z + 1) & (NZ - 1))
        below = jnp.where(z == LAST, 0, jnp.where(z < 2, NOWHERE, z - 1))
        beside = jnp.where(c == 0, above, below)
        if not first:
            return 4 * beside + 2 * (yh ^ 1) + c
        return 4 * jnp.where(j < 4, z, beside) + 2 * (yh ^ ((j >> 1) & 1)) + c

    for i in range(nq):
        block = query_block(i)
        per = pos_ref.shape[1] // tokens
        line = pos_ref[pl.ds(block // per, 1), :]
        row = line[:, :tokens]
        for n in range(1, per):
            row = jnp.where(block % per == n, line[:, n * tokens : (n + 1) * tokens], row)
        pos_s[i] = jnp.broadcast_to(jnp.concatenate([row] * groups, axis=1), (8, rows))
    for i in range(nq):
        q_copies[i].wait()
        for g in range(groups):
            q_s[i, g * tokens : (g + 1) * tokens, :] = flat_s[i, :, g * hd : (g + 1) * hd]
    if not first:
        for c in held_copies:
            c.wait()

    def scores_of(i, j, step):
        out = []
        for t in range(0, span, step):
            k = jnp.concatenate(
                [kv_s[j, hd:, u : u + hd] for u in range(t, t + step, hd)], axis=0
            )
            out.append(
                lax.dot_general(k, q_s[i], (((1,), (1,)), ((), ())), preferred_element_type=F32)
            )
        return out

    def safe_unit(i, j, ck):
        (s,) = scores_of(i, j, span)
        kpos = lax.broadcasted_iota(jnp.int32, (span, rows), 0) + ck * span
        pos = pos_s[i, :1, :]
        low = jnp.where(pos >= cut, cut, 0)
        s = jnp.where((kpos <= pos) & (kpos >= low), s, MASKED)
        s = s.reshape(span // 8, 8, rows)
        m_old = m_s[i]
        m_new = jnp.maximum(m_old, jnp.max(jnp.max(s, axis=0), axis=0, keepdims=True))
        fade = jnp.exp2((m_old - m_new) * scale2)
        p = jnp.exp2(s * scale2 - (m_new * scale2)[None])
        l_s[i] = l_s[i] * fade + jnp.sum(p, axis=0)
        acc_s[i] = acc_s[i] * fade[:1] + jnp.dot(
            kv_s[j, :hd, :], p.reshape(span, rows).astype(BF16), preferred_element_type=F32
        )
        m_s[i] = m_new

    def fast_unit(i, j):
        step = 2 * hd
        m_old = m_s[i]
        base = m_old * scale2
        top = m_old
        total = l_s[i]
        parts = []
        for s in scores_of(i, j, step):
            s = s.reshape(step // 8, 8, rows)
            top = jnp.maximum(top, jnp.max(s, axis=0))
            p = jnp.exp2(s * scale2 - base[None])
            total = total + jnp.sum(p, axis=0)
            parts.append(p.reshape(step, rows).astype(BF16))
        acc_t[...] = acc_s[i] + jnp.dot(
            kv_s[j, :hd, :], jnp.concatenate(parts, axis=0), preferred_element_type=F32
        )
        m_new = jnp.broadcast_to(jnp.max(top, axis=0, keepdims=True), (8, rows))
        climb = (m_new - m_old) * scale2
        fine = jnp.max(climb) < CLIMB

        @pl.when(fine)
        def _():
            fade = jnp.exp2(-climb)
            l_s[i] = total * fade
            acc_s[i] = acc_t[...] * fade[:1]
            m_s[i] = m_new

        return fine

    for i in range(nq):
        begun[i] = (jnp.max(m_s[i]) > 0.5 * FLOOR).astype(jnp.int32) if not first else jnp.int32(0)

    def one(n, carry):
        j = n // nq
        i = n % nq
        ck = key_block(j)
        cq = query_block(0)
        for n in range(1, nq):
            cq = jnp.where(i == n, query_block(n), cq)
        lent = (i == 1) & (z == LAST - 1)
        cq = jnp.where(lent & (j >= 4 if first else True), -1, cq)
        begin_k, end_k = ck * span, (ck + 1) * span
        begin_q, end_q = cq * span, (cq + 1) * span
        apart = (cut >= end_k) & (cut <= begin_q)
        whole = (ck < cq) & ((cut <= begin_k) | (cut >= end_q))
        some = (ck <= cq) & jnp.logical_not(apart)
        todo[0] = some.astype(jnp.int32)

        @pl.when(i == 0)
        def _():
            pltpu.make_async_copy(kv_s.at[j], kv_s.at[j], kv_sem.at[j]).wait()

        @pl.when(whole & (begun[i] == 0))
        def _():
            s = lax.dot_general(
                kv_s[j, hd:, :hd], q_s[i], (((1,), (1,)), ((), ())), preferred_element_type=F32
            )
            m_s[i] = jnp.broadcast_to(jnp.max(s, axis=0, keepdims=True), (8, rows))
            begun[i] = 1

        @pl.when(whole)
        def _():
            todo[0] = 1 - fast_unit(i, j).astype(jnp.int32)

        @pl.when(todo[0] > 0)
        def _():
            safe_unit(i, j, ck)
            begun[i] = 1

        return carry

    lax.fori_loop(0, nq * nk, one, 0)
    if not last:
        out_copies = [
            pltpu.make_async_copy((m_s, l_s, acc_s)[n % 3].at[n // 3], r, st_sem.at[n])
            for n, r in enumerate(outs)
        ]
        for c in out_copies:
            c.start()
        for c in out_copies:
            c.wait()
        return
    lane = lax.broadcasted_iota(jnp.int32, (tokens, hd), 1)
    for i in range(nq):
        total = jnp.sum(l_s[i], axis=0, keepdims=True)
        used = total > 0.0
        safe = jnp.where(used, total, 1.0)
        done = acc_s[i] * (1.0 / safe)
        level = jnp.where(used, m_s[i, :1, :] * scale2 + jnp.log2(safe), FLOOR)
        high = level.astype(BF16).astype(F32)
        mid = (level - high).astype(BF16).astype(F32)
        low = level - high - mid
        flag = jnp.where(used, 1.0, 0.0)
        stats = [high, mid, low, flag]
        table = jnp.concatenate(
            [v[:, g * tokens : (g + 1) * tokens] for v in stats for g in range(groups)]
            + [jnp.zeros((hd - 4 * groups, tokens), F32)],
            axis=0,
        )
        outs[i][:, groups * hd :] = table.T.astype(BF16)
        for g in range(groups):
            block = done[:, g * tokens : (g + 1) * tokens]
            outs[i][:, g * hd : (g + 1) * hd] = block.T.astype(BF16)


def flash(seg, pos, qs, spare, kvs, state, last):
    nq, nk = len(qs), len(kvs)
    tokens, width = qs[0].shape
    hd, span = kvs[0].shape[0] // 2, kvs[0].shape[1]
    groups = width // hd
    rows = groups * tokens
    scale2 = math.log2(math.e) * hd ** (-0.5)
    first = state is None
    state_types = [
        jax.ShapeDtypeStruct((8, rows), F32),
        jax.ShapeDtypeStruct((8, rows), F32),
        jax.ShapeDtypeStruct((hd, rows), F32),
    ]
    scratch = [
        pltpu.VMEM((nq, tokens, width), BF16),
        pltpu.VMEM((nq, rows, hd), BF16),
        pltpu.VMEM((nk, 2 * hd, span), BF16),
        pltpu.VMEM((nq, 8, rows), jnp.int32),
        pltpu.VMEM((hd, rows), F32),
        pltpu.SMEM((nq,), jnp.int32),
        pltpu.SMEM((1,), jnp.int32),
    ]
    scratch += [pltpu.VMEM((nq, *t.shape), t.dtype) for t in state_types]
    if last:
        outs = [jax.ShapeDtypeStruct((tokens, width + hd), BF16)] * nq
    else:
        outs = state_types * nq
    scratch += [
        pltpu.SemaphoreType.DMA((nq,)),
        pltpu.SemaphoreType.DMA((nk,)),
        pltpu.SemaphoreType.DMA((3 * nq,)),
        pltpu.VMEM(seg.shape, seg.dtype),
        pltpu.VMEM(pos.shape, pos.dtype),
        pltpu.SemaphoreType.DMA((2,)),
    ]
    return pl.pallas_call(
        functools.partial(flash_kernel, nq, nk, first, last, groups, rows, scale2),
        out_shape=outs,
        in_specs=[ANY] * (3 + nq + nk + (0 if first else 3 * nq)),
        out_specs=[VMEM if last else ANY] * len(outs),
        scratch_shapes=scratch,
        compiler_params=pltpu.CompilerParams(vmem_limit_bytes=FLASH_LIMIT),
        cost_estimate=cost(1e6, 1e5),
    )(seg, pos, *qs, spare, *kvs, *(() if first else state))


def combine_kernel(groups, *refs):
    parts, out = refs[:-1], refs[-1]
    tokens, width = out.shape
    hd = width // groups
    stats = [r[:, width:].astype(F32) for r in parts]
    for g in range(groups):
        levels = []
        for s in stats:
            level = (
                s[:, g : g + 1]
                + s[:, groups + g : groups + g + 1]
                + s[:, 2 * groups + g : 2 * groups + g + 1]
            )
            levels.append(jnp.where(s[:, 3 * groups + g : 3 * groups + g + 1] > 0.0, level, FLOOR))
        top = functools.reduce(jnp.maximum, levels)
        shares = [jnp.where(x > FLOOR, jnp.exp2(x - top), 0.0) for x in levels]
        total = functools.reduce(lambda a, b: a + b, shares)
        summed = 0.0
        for r, share in zip(parts, shares):
            summed = summed + r[:, g * hd : (g + 1) * hd].astype(F32) * share
        out[:, g * hd : (g + 1) * hd] = (summed / total).astype(BF16)


def combine(parts, groups):
    tokens, wide = parts[0].shape
    hd = wide // (groups + 1)
    return pl.pallas_call(
        functools.partial(combine_kernel, groups),
        out_shape=jax.ShapeDtypeStruct((tokens, groups * hd), BF16),
        in_specs=[VMEM] * len(parts),
        out_specs=VMEM,
        compiler_params=pltpu.CompilerParams(vmem_limit_bytes=LIMIT),
        cost_estimate=cost(1e6, 1e6),
    )(*parts)


def project_kernel(nb, nw, *refs):
    ids = refs[0]
    blocks = refs[1 : 1 + nb]
    ws = refs[1 + nb : 1 + nb + nw]
    outs = refs[1 + nb + nw : -1]
    rows_s = refs[-1]
    tokens = blocks[0].shape[0]
    cols = ws[0].shape[1]
    for b in range(nb):
        rows_s[pl.ds(pl.multiple_of(ids[b] * tokens, tokens), tokens), :] = blocks[b][...]
    rows = rows_s[...]
    for w in range(nw):
        y = jnp.dot(rows, ws[w][...], preferred_element_type=F32).astype(BF16)
        for n, out in enumerate(outs):
            for half in range(2):
                lo = (2 * n + half) * tokens
                out[half, :, w * cols : (w + 1) * cols] = y[lo : lo + tokens]


def project(slots, blocks, ws, nx):
    tokens, width = blocks[0].shape
    nb, nw = len(blocks), len(ws)
    cols = ws[0].shape[1]
    out = jax.ShapeDtypeStruct((2, tokens, nw * cols), BF16)
    return pl.pallas_call(
        functools.partial(project_kernel, nb, nw),
        out_shape=[out] * nx,
        in_specs=[SMEM] + [VMEM] * (nb + nw),
        out_specs=[VMEM] * nx,
        scratch_shapes=[pltpu.VMEM((nb * tokens, width), BF16)],
        compiler_params=pltpu.CompilerParams(vmem_limit_bytes=LIMIT),
        cost_estimate=cost(2 * nb * tokens * width * nw * cols, 4e6),
    )(slots, *blocks, *ws)


def swap(array, axis):
    return lax.ppermute(array, axis, [(0, 1), (1, 0)])


def useful(plane, owner):
    return owner >= plane - 1 or plane == NZ - 1


def fetch(array, k, trim):
    pairs = [((z + k) % NZ, z) for z in range(NZ) if not trim or useful(z, (z + k) % NZ)]
    return lax.ppermute(array, "z", pairs)


def give(array, k):
    pairs = [(z, (z + k) % NZ) for z in range(NZ) if useful(z, (z + k) % NZ)]
    return lax.ppermute(array, "z", pairs)


def lender(z, c):
    if c == 0:
        return None if z == LAST - 2 else (z + 1) % NZ
    return {0: None, 1: None, LAST: 0}.get(z, z - 1)


def beside(array):
    pairs = [
        ((lender(z, c) * 2 + y) * 2 + c, (z * 2 + y) * 2 + c)
        for z in range(NZ)
        for y in range(2)
        for c in range(2)
        if lender(z, c) is not None
    ]
    return lax.ppermute(array, ("z", "yh", "core"), pairs)


def per_device(
    queries, latent_keys, latent_values, key_basis, value_basis, out_weight, positions, key_segments
):
    z, yh, core = lax.axis_index("z"), lax.axis_index("yh"), lax.axis_index("core")
    yl, x = lax.axis_index("yl"), lax.axis_index("x")
    tokens, width = queries.shape
    hd = key_basis.shape[2]
    groups = width // hd
    span = latent_keys.shape[0]
    kv = rebuild(latent_keys, latent_values, key_basis, value_basis)
    lent, kv = lax.optimization_barrier((queries, kv))
    q_far = fetch(lent, 4, True)
    q_down = fetch(lent, 6, True)
    spare = lax.ppermute(lent, "z", [(LAST, LAST - 1)])
    qs = [queries, fetch(lent, 2, True), q_down, q_far]
    kv_y = swap(kv, "yh")
    kv_far = beside(kv)

    def both_cores(array):
        return [array, swap(array, "core")]

    seg, pos = key_segments.reshape(-1, 128), positions.reshape(-1, 128)
    kv, kv_y, kv_far, spare, *qs = lax.optimization_barrier((kv, kv_y, kv_far, spare, *qs))
    kv_far_y = swap(kv_far, "yh")
    kvs = both_cores(kv) + both_cores(kv_y) + both_cores(kv_far)
    state = flash(seg, pos, qs, spare, kvs, None, False)
    kv_far_y, out_weight, *state = lax.optimization_barrier((kv_far_y, out_weight, *state))
    w_y = swap(out_weight, "yh")
    parts = flash(seg, pos, qs, spare, both_cores(kv_far_y), state, True)
    back = [parts[0]] + [give(parts[n], SHIFTS[n]) for n in (3, 1, 2)]
    back += [lax.ppermute(parts[1], "z", [(LAST - 1, LAST)])]
    attended = combine(back, groups)
    w_y, attended = lax.optimization_barrier((w_y, attended))
    ws = [out_weight, swap(out_weight, "core"), w_y, swap(w_y, "core")]

    up2, down2, far = [fetch(attended, k, False) for k in SHIFTS[1:]]
    above = fetch(jnp.concatenate([attended, up2], axis=0), 1, False)
    below = fetch(jnp.concatenate([attended, down2], axis=0), NZ - 1, False)
    blocks = [attended, above[:tokens], below[:tokens], up2, down2, far]
    blocks += [above[tokens:], below[tokens:]]
    planes = [(z + k) % NZ for k in (0, 1, 7, 2, 6, 4, 3, 5)]
    slots = [2 * ((p % 4 - x) % 4) + ((p // 4) ^ yl) for p in planes]
    outs = project(jnp.stack(slots).astype(jnp.int32), blocks, ws, 4)

    def along_x(array, k):
        return lax.ppermute(array, "x", [(n, (n + k) % 4) for n in range(4)])

    summed = outs[0].astype(F32)
    for k in (1, 2, 3):
        summed = summed + along_x(outs[k], k).astype(F32)
    half = summed.shape[2] // 2

    def along_y(array, a, b):
        pairs = [(2 * m + n, 2 * (m ^ a) + (n ^ b)) for m in range(2) for n in range(2)]
        return lax.ppermute(array, ("yl", "yh"), pairs)

    sent = summed.astype(BF16)
    from_l = along_y(sent[1, :, :half], 1, 0)
    from_h = along_y(sent[0, :, half:], 0, 1)
    from_lh = along_y(sent[1, :, half:], 1, 1)
    mine = (summed[0, :, :half] + from_l.astype(F32)).astype(BF16)
    theirs = (from_h.astype(F32) + from_lh.astype(F32)).astype(BF16)
    both = jnp.stack([jnp.where(yh == 0, mine, theirs), jnp.where(yh == 0, theirs, mine)])
    cols = half // 2
    here = both[:, :, :cols]
    there = swap(both[:, :, cols:], "core")
    rows = jnp.stack([jnp.where(core == 0, here, there), jnp.where(core == 0, there, here)], axis=1)
    return rows.reshape(-1, cols)


def solution(mesh):
    fine = Mesh(mesh.devices.reshape(2, 4, NZ, 2, 2), ("yl", "x", "z", "yh", "core"))
    head, ctx = ("yl", "x"), ("z", "yh", "core")
    placed = (
        P(ctx, head),
        P(ctx, head),
        P(ctx, head),
        P(head, None, None),
        P(head, None, None),
        P(head, ctx),
        P(),
        P(),
    )
    return jax.shard_map(
        per_device, mesh=fine, in_specs=placed, out_specs=P(head, ctx), check_vma=False
    )
```

```python
import functools
import math

import jax
import jax.numpy as jnp
import numpy as np
from jax import lax
from jax.experimental import pallas as pl
from jax.experimental.pallas import tpu as pltpu
from jax.sharding import Mesh, PartitionSpec as P

NZ = 8
LAST = NZ - 1
NOWHERE = 1 << 16
FLOOR = -1e30
MASKED = -2e38
CLIMB = 40.0
F32 = jnp.float32
BF16 = jnp.bfloat16
VMEM = pl.BlockSpec(memory_space=pltpu.VMEM)
SMEM = pl.BlockSpec(memory_space=pltpu.SMEM)
ANY = pl.BlockSpec(memory_space=pl.ANY)
LIMIT = 24 * 1024 * 1024
FLASH_LIMIT = 28 * 1024 * 1024
REBUILD_LIMIT = 60 * 1024 * 1024
SHIFTS = (0, 2, 6, 4)


def cost(flops, moved):
    return pl.CostEstimate(flops=int(flops), bytes_accessed=int(moved), transcendentals=0)


def rebuild_kernel(lk_in, lv_in, bk_in, bv_in, kv_ref, lk_ref, lv_ref, bk_ref, bv_ref, sems):
    pairs = [(lk_in, lk_ref), (bk_in, bk_ref), (lv_in, lv_ref), (bv_in, bv_ref)]
    copies = [pltpu.make_async_copy(a, b, sems.at[n]) for n, (a, b) in enumerate(pairs)]
    for c in copies:
        c.start()
    for c in copies:
        c.wait()
    hd = bk_ref.shape[2]
    values = lax.dot_general(
        bv_ref[0], lv_ref[...], (((0,), (1,)), ((), ())), preferred_element_type=F32
    )
    kv_ref[:hd, :] = values.astype(BF16)
    for t in range(lk_ref.shape[0] // hd):
        part = slice(t * hd, (t + 1) * hd)
        keys = jnp.dot(lk_ref[part, :], bk_ref[0], preferred_element_type=F32)
        kv_ref[hd:, part] = keys.astype(BF16)


def rebuild(lk, lv, bk, bv):
    rows, hd = lk.shape[0], bk.shape[2]
    arrays = (lk, lv, bk, bv)
    return pl.pallas_call(
        rebuild_kernel,
        out_shape=jax.ShapeDtypeStruct((2 * hd, rows), BF16),
        in_specs=[ANY] * 4,
        out_specs=VMEM,
        scratch_shapes=[pltpu.VMEM(t.shape, t.dtype) for t in arrays]
        + [pltpu.SemaphoreType.DMA((4,))],
        compiler_params=pltpu.CompilerParams(vmem_limit_bytes=REBUILD_LIMIT),
        cost_estimate=cost(4 * rows * hd * hd, 8 * rows * hd),
    )(*arrays)


def flash_kernel(nq, nk, first, last, groups, rows, scale2, *refs):
    seg_in, pos_in = refs[0], refs[1]
    qs = refs[2 : 2 + nq]
    spare = refs[2 + nq]
    kvs = refs[3 + nq : 3 + nq + nk]
    at = 3 + nq + nk
    z, yh, core = lax.axis_index("z"), lax.axis_index("yh"), lax.axis_index("core")
    if not first:
        held = refs[at : at + 3 * nq]
        at += 3 * nq
    if last:
        outs = refs[at : at + nq]
        at += nq
    else:
        outs = refs[at : at + 3 * nq]
        at += 3 * nq
    flat_s, q_s, kv_s, pos_s, acc_t, begun, m_s, l_s, acc_s, *rest = refs[at:]
    q_sem, kv_sem, st_sem, seg_ref, pos_ref, small_sem = rest
    hd = kvs[0].shape[0] // 2
    span = kvs[0].shape[1]
    tokens = qs[0].shape[0]
    kv_copies = [pltpu.make_async_copy(kvs[j], kv_s.at[j], kv_sem.at[j]) for j in range(nk)]
    q_copies = [pltpu.make_async_copy(qs[i], flat_s.at[i], q_sem.at[i]) for i in range(nq)]
    small = [
        pltpu.make_async_copy(seg_in, seg_ref, small_sem.at[0]),
        pltpu.make_async_copy(pos_in, pos_ref, small_sem.at[1]),
    ]
    for c in small + q_copies[:1] + q_copies[2:] + kv_copies:
        c.start()

    @pl.when(z == LAST - 1)
    def _():
        pltpu.make_async_copy(spare, flat_s.at[1], q_sem.at[1]).start()

    @pl.when(z != LAST - 1)
    def _():
        q_copies[1].start()

    if first:
        m_s[...] = jnp.full_like(m_s, FLOOR)
        l_s[...] = jnp.zeros_like(l_s)
        acc_s[...] = jnp.zeros_like(acc_s)
    else:
        held_copies = [
            pltpu.make_async_copy(r, (m_s, l_s, acc_s)[n % 3].at[n // 3], st_sem.at[n])
            for n, r in enumerate(held)
        ]
        for c in held_copies:
            c.start()
    for c in small:
        c.wait()
    cut = jnp.sum(jnp.where(seg_ref[...] == 0, 1.0, 0.0)).astype(jnp.int32)

    def query_block(i):
        plane = (z + SHIFTS[i]) & (NZ - 1)
        if i == 1:
            plane = jnp.where(z == LAST - 1, LAST, plane)
        return 4 * plane + 2 * yh + core

    def key_block(j):
        c = core ^ (j & 1)
        above = jnp.where(z == LAST - 2, NOWHERE, (z + 1) & (NZ - 1))
        below = jnp.where(z == LAST, 0, jnp.where(z < 2, NOWHERE, z - 1))
        beside = jnp.where(c == 0, above, below)
        if not first:
            return 4 * beside + 2 * (yh ^ 1) + c
        return 4 * jnp.where(j < 4, z, beside) + 2 * (yh ^ ((j >> 1) & 1)) + c

    for i in range(nq):
        block = query_block(i)
        per = pos_ref.shape[1] // tokens
        line = pos_ref[pl.ds(block // per, 1), :]
        row = line[:, :tokens]
        for n in range(1, per):
            row = jnp.where(block % per == n, line[:, n * tokens : (n + 1) * tokens], row)
        pos_s[i] = jnp.broadcast_to(jnp.concatenate([row] * groups, axis=1), (8, rows))
    for i in range(nq):
        q_copies[i].wait()
        for g in range(groups):
            q_s[i, g * tokens : (g + 1) * tokens, :] = flat_s[i, :, g * hd : (g + 1) * hd]
    if not first:
        for c in held_copies:
            c.wait()

    def scores_of(i, j, step):
        out = []
        for t in range(0, span, step):
            k = jnp.concatenate(
                [kv_s[j, hd:, u : u + hd] for u in range(t, t + step, hd)], axis=0
            )
            out.append(
                lax.dot_general(k, q_s[i], (((1,), (1,)), ((), ())), preferred_element_type=F32)
            )
        return out

    def safe_unit(i, j, ck):
        (s,) = scores_of(i, j, span)
        kpos = lax.broadcasted_iota(jnp.int32, (span, rows), 0) + ck * span
        pos = pos_s[i, :1, :]
        low = jnp.where(pos >= cut, cut, 0)
        s = jnp.where((kpos <= pos) & (kpos >= low), s, MASKED)
        s = s.reshape(span // 8, 8, rows)
        m_old = m_s[i]
        m_new = jnp.maximum(m_old, jnp.max(jnp.max(s, axis=0), axis=0, keepdims=True))
        fade = jnp.exp2((m_old - m_new) * scale2)
        p = jnp.exp2(s * scale2 - (m_new * scale2)[None])
        l_s[i] = l_s[i] * fade + jnp.sum(p, axis=0)
        acc_s[i] = acc_s[i] * fade[:1] + jnp.dot(
            kv_s[j, :hd, :], p.reshape(span, rows).astype(BF16), preferred_element_type=F32
        )
        m_s[i] = m_new

    def fast_unit(i, j):
        step = 2 * hd
        m_old = m_s[i]
        base = m_old * scale2
        top = m_old
        total = l_s[i]
        parts = []
        for s in scores_of(i, j, step):
            s = s.reshape(step // 8, 8, rows)
            top = jnp.maximum(top, jnp.max(s, axis=0))
            p = jnp.exp2(s * scale2 - base[None])
            total = total + jnp.sum(p, axis=0)
            parts.append(p.reshape(step, rows).astype(BF16))
        acc_t[...] = acc_s[i] + jnp.dot(
            kv_s[j, :hd, :], jnp.concatenate(parts, axis=0), preferred_element_type=F32
        )
        m_new = jnp.broadcast_to(jnp.max(top, axis=0, keepdims=True), (8, rows))
        climb = (m_new - m_old) * scale2
        fine = jnp.max(climb) < CLIMB

        @pl.when(fine)
        def _():
            fade = jnp.exp2(-climb)
            l_s[i] = total * fade
            acc_s[i] = acc_t[...] * fade[:1]
            m_s[i] = m_new

        return fine

    for i in range(nq):
        begun[i] = (jnp.max(m_s[i]) > 0.5 * FLOOR).astype(jnp.int32) if not first else jnp.int32(0)

    asked = [query_block(n) for n in range(nq)]

    def one(n, carry):
        j = lax.div(n, jnp.int32(nq))
        i = lax.rem(n, jnp.int32(nq))
        ck = key_block(j)
        cq = asked[0]
        for m in range(1, nq):
            cq = jnp.where(i == m, asked[m], cq)
        lent = (i == 1) & (z == LAST - 1)
        cq = jnp.where(lent & (j >= 4 if first else True), -1, cq)
        begin_k, end_k = ck * span, (ck + 1) * span
        begin_q, end_q = cq * span, (cq + 1) * span
        apart = (cut >= end_k) & (cut <= begin_q)
        whole = (ck < cq) & ((cut <= begin_k) | (cut >= end_q))
        some = (ck <= cq) & jnp.logical_not(apart)

        @pl.when(i == 0)
        def _():
            pltpu.make_async_copy(kv_s.at[j], kv_s.at[j], kv_sem.at[j]).wait()

        @pl.when(whole & (begun[i] == 0))
        def _():
            s = lax.dot_general(
                kv_s[j, hd:, :hd], q_s[i], (((1,), (1,)), ((), ())), preferred_element_type=F32
            )
            m_s[i] = jnp.broadcast_to(jnp.max(s, axis=0, keepdims=True), (8, rows))
            begun[i] = 1

        left = lax.cond(
            whole,
            lambda: 1 - fast_unit(i, j).astype(jnp.int32),
            lambda: some.astype(jnp.int32),
        )

        @pl.when(left > 0)
        def _():
            safe_unit(i, j, ck)
            begun[i] = 1

        return carry

    lax.fori_loop(0, nq * nk, one, 0)
    if not last:
        out_copies = [
            pltpu.make_async_copy((m_s, l_s, acc_s)[n % 3].at[n // 3], r, st_sem.at[n])
            for n, r in enumerate(outs)
        ]
        for c in out_copies:
            c.start()
        for c in out_copies:
            c.wait()
        return
    lane = lax.broadcasted_iota(jnp.int32, (tokens, hd), 1)
    for i in range(nq):
        total = jnp.sum(l_s[i], axis=0, keepdims=True)
        used = total > 0.0
        safe = jnp.where(used, total, 1.0)
        done = acc_s[i] * (1.0 / safe)
        level = jnp.where(used, m_s[i, :1, :] * scale2 + jnp.log2(safe), FLOOR)
        high = level.astype(BF16).astype(F32)
        mid = (level - high).astype(BF16).astype(F32)
        low = level - high - mid
        flag = jnp.where(used, 1.0, 0.0)
        stats = [high, mid, low, flag]
        table = jnp.concatenate(
            [v[:, g * tokens : (g + 1) * tokens] for v in stats for g in range(groups)]
            + [jnp.zeros((hd - 4 * groups, tokens), F32)],
            axis=0,
        )
        outs[i][:, groups * hd :] = table.T.astype(BF16)
        for g in range(groups):
            block = done[:, g * tokens : (g + 1) * tokens]
            outs[i][:, g * hd : (g + 1) * hd] = block.T.astype(BF16)


def flash(seg, pos, qs, spare, kvs, state, last):
    nq, nk = len(qs), len(kvs)
    tokens, width = qs[0].shape
    hd, span = kvs[0].shape[0] // 2, kvs[0].shape[1]
    groups = width // hd
    rows = groups * tokens
    scale2 = math.log2(math.e) * hd ** (-0.5)
    first = state is None
    state_types = [
        jax.ShapeDtypeStruct((8, rows), F32),
        jax.ShapeDtypeStruct((8, rows), F32),
        jax.ShapeDtypeStruct((hd, rows), F32),
    ]
    scratch = [
        pltpu.VMEM((nq, tokens, width), BF16),
        pltpu.VMEM((nq, rows, hd), BF16),
        pltpu.VMEM((nk, 2 * hd, span), BF16),
        pltpu.VMEM((nq, 8, rows), jnp.int32),
        pltpu.VMEM((hd, rows), F32),
        pltpu.SMEM((nq,), jnp.int32),
    ]
    scratch += [pltpu.VMEM((nq, *t.shape), t.dtype) for t in state_types]
    if last:
        outs = [jax.ShapeDtypeStruct((tokens, width + hd), BF16)] * nq
    else:
        outs = state_types * nq
    scratch += [
        pltpu.SemaphoreType.DMA((nq,)),
        pltpu.SemaphoreType.DMA((nk,)),
        pltpu.SemaphoreType.DMA((3 * nq,)),
        pltpu.VMEM(seg.shape, seg.dtype),
        pltpu.VMEM(pos.shape, pos.dtype),
        pltpu.SemaphoreType.DMA((2,)),
    ]
    return pl.pallas_call(
        functools.partial(flash_kernel, nq, nk, first, last, groups, rows, scale2),
        out_shape=outs,
        in_specs=[ANY] * (3 + nq + nk + (0 if first else 3 * nq)),
        out_specs=[VMEM if last else ANY] * len(outs),
        scratch_shapes=scratch,
        compiler_params=pltpu.CompilerParams(vmem_limit_bytes=FLASH_LIMIT),
        cost_estimate=cost(1e6, 1e5),
    )(seg, pos, *qs, spare, *kvs, *(() if first else state))


def combine_kernel(groups, *refs):
    parts, out = refs[:-1], refs[-1]
    tokens, width = out.shape
    hd = width // groups
    stats = [r[:, width:].astype(F32) for r in parts]
    for g in range(groups):
        levels = []
        for s in stats:
            level = (
                s[:, g : g + 1]
                + s[:, groups + g : groups + g + 1]
                + s[:, 2 * groups + g : 2 * groups + g + 1]
            )
            levels.append(jnp.where(s[:, 3 * groups + g : 3 * groups + g + 1] > 0.0, level, FLOOR))
        top = functools.reduce(jnp.maximum, levels)
        shares = [jnp.where(x > FLOOR, jnp.exp2(x - top), 0.0) for x in levels]
        total = functools.reduce(lambda a, b: a + b, shares)
        summed = 0.0
        for r, share in zip(parts, shares):
            summed = summed + r[:, g * hd : (g + 1) * hd].astype(F32) * share
        out[:, g * hd : (g + 1) * hd] = (summed / total).astype(BF16)


def combine(parts, groups):
    tokens, wide = parts[0].shape
    hd = wide // (groups + 1)
    return pl.pallas_call(
        functools.partial(combine_kernel, groups),
        out_shape=jax.ShapeDtypeStruct((tokens, groups * hd), BF16),
        in_specs=[VMEM] * len(parts),
        out_specs=VMEM,
        compiler_params=pltpu.CompilerParams(vmem_limit_bytes=LIMIT),
        cost_estimate=cost(1e6, 1e6),
    )(*parts)


def project_kernel(nb, nw, *refs):
    ids = refs[0]
    blocks = refs[1 : 1 + nb]
    ws = refs[1 + nb : 1 + nb + nw]
    outs = refs[1 + nb + nw : -1]
    rows_s = refs[-1]
    tokens = blocks[0].shape[0]
    cols = ws[0].shape[1]
    for b in range(nb):
        rows_s[pl.ds(pl.multiple_of(ids[b] * tokens, tokens), tokens), :] = blocks[b][...]
    rows = rows_s[...]
    for w in range(nw):
        y = jnp.dot(rows, ws[w][...], preferred_element_type=F32).astype(BF16)
        for n, out in enumerate(outs):
            for half in range(2):
                lo = (2 * n + half) * tokens
                out[half, :, w * cols : (w + 1) * cols] = y[lo : lo + tokens]


def project(slots, blocks, ws, nx):
    tokens, width = blocks[0].shape
    nb, nw = len(blocks), len(ws)
    cols = ws[0].shape[1]
    out = jax.ShapeDtypeStruct((2, tokens, nw * cols), BF16)
    return pl.pallas_call(
        functools.partial(project_kernel, nb, nw),
        out_shape=[out] * nx,
        in_specs=[SMEM] + [VMEM] * (nb + nw),
        out_specs=[VMEM] * nx,
        scratch_shapes=[pltpu.VMEM((nb * tokens, width), BF16)],
        compiler_params=pltpu.CompilerParams(vmem_limit_bytes=LIMIT),
        cost_estimate=cost(2 * nb * tokens * width * nw * cols, 4e6),
    )(slots, *blocks, *ws)


def swap(array, axis):
    return lax.ppermute(array, axis, [(0, 1), (1, 0)])


def useful(plane, owner):
    return owner >= plane - 1 or plane == NZ - 1


def fetch(array, k, trim):
    pairs = [((z + k) % NZ, z) for z in range(NZ) if not trim or useful(z, (z + k) % NZ)]
    return lax.ppermute(array, "z", pairs)


def give(array, k):
    pairs = [(z, (z + k) % NZ) for z in range(NZ) if useful(z, (z + k) % NZ)]
    return lax.ppermute(array, "z", pairs)


def lender(z, c):
    if c == 0:
        return None if z == LAST - 2 else (z + 1) % NZ
    return {0: None, 1: None, LAST: 0}.get(z, z - 1)


def beside(array):
    pairs = [
        ((lender(z, c) * 2 + y) * 2 + c, (z * 2 + y) * 2 + c)
        for z in range(NZ)
        for y in range(2)
        for c in range(2)
        if lender(z, c) is not None
    ]
    return lax.ppermute(array, ("z", "yh", "core"), pairs)


def per_device(
    queries, latent_keys, latent_values, key_basis, value_basis, out_weight, positions, key_segments
):
    z, yh, core = lax.axis_index("z"), lax.axis_index("yh"), lax.axis_index("core")
    yl, x = lax.axis_index("yl"), lax.axis_index("x")
    tokens, width = queries.shape
    hd = key_basis.shape[2]
    groups = width // hd
    span = latent_keys.shape[0]
    kv = rebuild(latent_keys, latent_values, key_basis, value_basis)
    lent = queries
    q_far = fetch(lent, 4, True)
    q_down = fetch(lent, 6, True)
    spare = lax.ppermute(lent, "z", [(LAST, LAST - 1)])
    qs = [queries, fetch(lent, 2, True), q_down, q_far]
    kv_y = swap(kv, "yh")
    kv_far = beside(kv)

    def both_cores(array):
        return [array, swap(array, "core")]

    seg, pos = key_segments.reshape(-1, 128), positions.reshape(-1, 128)
    q_up, q_down, q_far = qs[1:]
    q_far, q_up, q_down, kv, kv_y, kv_far, spare = lax.optimization_barrier(
        (q_far, q_up, q_down, kv, kv_y, kv_far, spare)
    )
    qs = [queries, q_up, q_down, q_far]
    kv_far_y = swap(kv_far, "yh")
    kvs = both_cores(kv) + both_cores(kv_y) + both_cores(kv_far)
    state = flash(seg, pos, qs, spare, kvs, None, False)
    kv_far_y, out_weight, *state = lax.optimization_barrier((kv_far_y, out_weight, *state))
    w_y = swap(out_weight, "yh")
    parts = flash(seg, pos, qs, spare, both_cores(kv_far_y), state, True)
    back = [parts[0]] + [give(parts[n], SHIFTS[n]) for n in (3, 1, 2)]
    back += [lax.ppermute(parts[1], "z", [(LAST - 1, LAST)])]
    attended = combine(back, groups)
    w_y, attended = lax.optimization_barrier((w_y, attended))
    ws = [out_weight, swap(out_weight, "core"), w_y, swap(w_y, "core")]

    up, down = fetch(attended, 1, False), fetch(attended, NZ - 1, False)
    up2, down2, far = [fetch(attended, k, False) for k in SHIFTS[1:]]
    blocks = [attended, up, down, up2, down2, far, fetch(up2, 1, False), fetch(down2, NZ - 1, False)]
    planes = [(z + k) % NZ for k in (0, 1, 7, 2, 6, 4, 3, 5)]
    slots = [2 * ((p % 4 - x) % 4) + ((p // 4) ^ yl) for p in planes]
    outs = project(jnp.stack(slots).astype(jnp.int32), blocks, ws, 4)

    def along_x(array, k):
        return lax.ppermute(array, "x", [(n, (n + k) % 4) for n in range(4)])

    summed = outs[0].astype(F32)
    for k in (1, 2, 3):
        summed = summed + along_x(outs[k], k).astype(F32)
    half = summed.shape[2] // 2

    def along_y(array, a, b):
        pairs = [(2 * m + n, 2 * (m ^ a) + (n ^ b)) for m in range(2) for n in range(2)]
        return lax.ppermute(array, ("yl", "yh"), pairs)

    sent = summed.astype(BF16)
    from_l = along_y(sent[1, :, :half], 1, 0)
    from_h = along_y(sent[0, :, half:], 0, 1)
    from_lh = along_y(sent[1, :, half:], 1, 1)
    mine = (summed[0, :, :half] + from_l.astype(F32)).astype(BF16)
    theirs = (from_h.astype(F32) + from_lh.astype(F32)).astype(BF16)
    both = jnp.stack([jnp.where(yh == 0, mine, theirs), jnp.where(yh == 0, theirs, mine)])
    cols = half // 2
    here = both[:, :, :cols]
    there = swap(both[:, :, cols:], "core")
    rows = jnp.stack([jnp.where(core == 0, here, there), jnp.where(core == 0, there, here)], axis=1)
    return rows.reshape(-1, cols)


def solution(mesh):
    fine = Mesh(mesh.devices.reshape(2, 4, NZ, 2, 2), ("yl", "x", "z", "yh", "core"))
    head, ctx = ("yl", "x"), ("z", "yh", "core")
    placed = (
        P(ctx, head),
        P(ctx, head),
        P(ctx, head),
        P(head, None, None),
        P(head, None, None),
        P(head, ctx),
        P(),
        P(),
    )
    return jax.shard_map(
        per_device, mesh=fine, in_specs=placed, out_specs=P(head, ctx), check_vma=False
    )
```
